256 devices in a mesh: row: 32 (over x_hi, z, core), col: 8 (over x_lo, y).
Axes of the slice: x: 4 (x_hi: 2, x_lo: 2; x = x_hi * 2 + x_lo), y: 4, z: 8, core: 2. Of those that a mesh axis runs over, the one named last changes fastest.
Arguments:
- queries: bfloat16 [131072, 256], P(('row', 'col')), may hold values from -36 to 36
- key_rows: bfloat16 [131072, 128], P(('row', 'col')), may hold values from -16 to 16
- value_rows: bfloat16 [131072, 128], P(('row', 'col')), may hold values from -6 to 6
- out_grad: bfloat16 [131072, 256], P(('row', 'col')), may hold values from -6 to 6
- link_mask: int32 [256, 5], P(('row', 'col')), may hold values 0 or 1
Outputs:
- attention_out: bfloat16 [131072, 256], P(('row', 'col'))
- query_grad: bfloat16 [131072, 256], P(('row', 'col'))
- key_grad: bfloat16 [131072, 128], P(('row', 'col'))
- value_grad: bfloat16 [131072, 128], P(('row', 'col'))
The draws below stay inside these ranges and needn't reach their ends.
All inputs are finite; a program needn't handle non-finite values. No bound on the sum of `link_mask` on one device may be relied on, other than what follows from the above.
Results may differ from the reference program's by a relative error of at most 0.025.
Values may be sent and summed in bfloat16 or wider, within the bound.
A program may use at most 64 MiB of HBM per device.

```python
import math
import jax
import jax.numpy as jnp
from jax import lax

TOK_DEV = 512
HD = 128
HQ = 2
LEVELS = 5
BLOCKS = 256
SEQ = 131072


def powers_of_two(exponents):
    table = jnp.array([2.0 ** power for power in range(-8, 0)], jnp.float32)
    return table[exponents + 8]


def coded_rows(key, salt, lead_shape, lowest, highest):
    base = jax.random.fold_in(key, salt)
    full_shape = lead_shape + (HD,)
    side_shape = lead_shape + (1,)
    first = jax.random.randint(jax.random.fold_in(base, 1), full_shape, -63, 64, jnp.int32)
    second = jax.random.randint(jax.random.fold_in(base, 2), full_shape, -63, 64, jnp.int32)
    column = jax.random.randint(jax.random.fold_in(base, 3), side_shape, 0, HD, jnp.int32)
    signs = 2 * jax.random.randint(jax.random.fold_in(base, 4), side_shape, 0, 2, jnp.int32) - 1
    exponents = jax.random.randint(jax.random.fold_in(base, 5), side_shape, lowest, highest + 1, jnp.int32)
    columns = jnp.arange(HD, dtype=jnp.int32)
    codes = jnp.where(columns == column, 127 * signs, first + second)
    return (codes, exponents)


def paired_rows(key):
    lowest, highest = (-6, -5)
    key_codes, key_expo = coded_rows(key, 101, (SEQ,), lowest, highest)
    query_codes, query_expo = coded_rows(key, 102, (SEQ, HQ), lowest, highest)
    key_out = key_codes.astype(jnp.float32) * powers_of_two(key_expo)
    query_out = (query_codes.astype(jnp.float32) * powers_of_two(query_expo)).reshape(SEQ, HQ * HD)
    return (key_out, query_out)


def draw_queries(key, part):
    return paired_rows(key)[1].astype(jnp.bfloat16)


def draw_key_rows(key, part):
    return paired_rows(key)[0].astype(jnp.bfloat16)


def set_ends(values, key, least, high):
    extent = values.shape
    spot = [jax.random.randint(jax.random.fold_in(key, axis), (), 0, extent[axis]) for axis in range(len(extent))]
    values = values.at[tuple(spot)].set(least)
    longest = extent.index(max(extent))
    spot[longest] = (spot[longest] + 1) % extent[longest]
    return values.at[tuple(spot)].set(high)


def levels(key, shape, pieces, low, high):
    def one(dim, parts):
        steps = jax.random.uniform(jax.random.fold_in(jax.random.fold_in(key, 6), dim), (parts,), jnp.float32, low / len(pieces), high / len(pieces))
        return jnp.repeat(jnp.exp(steps), shape[dim] // parts).reshape((-1,) + (1,) * (len(shape) - dim - 1))

    level = one(*pieces[0])
    for cut in pieces[1:]:
        level = level * one(*cut)
    return level


def bell_draw(own_key, shape, spread, reach, split=(), kind=jnp.bfloat16):
    result = jax.random.normal(own_key, shape, jnp.float32) * spread
    if len(split) > 0:
        result = levels(own_key, shape, split, -0.22, 0.18) * result
    return jnp.clip(result, min=-reach, max=reach).astype(kind)


def setup_inputs(seed: int = 0) -> dict:
    key_of = jax.random.split(jax.random.key(seed), 6)
    queries = draw_queries(jax.random.fold_in(key_of[5], 71), 0)
    key_rows = draw_key_rows(jax.random.fold_in(key_of[5], 71), 0)
    value_rows = bell_draw(key_of[2], (SEQ, HD), 1.0, 6.0, ((0, 256),))
    out_grad = bell_draw(key_of[3], (SEQ, HQ * HD), 1.0, 6.0, ((0, 256),))
    link_mask = set_ends((jax.random.randint(key_of[4], (BLOCKS, LEVELS), 0, 4) < 3).astype(jnp.int32), jax.random.fold_in(key_of[4], 1), 0, 1)
    return dict(queries=queries, key_rows=key_rows, value_rows=value_rows, out_grad=out_grad, link_mask=link_mask)


scale_eps = 1e-06

def quantize(values):
    largest = lax.optimization_barrier(jnp.max(jnp.abs(values), axis=-1))
    scales = (largest + scale_eps).astype(jnp.bfloat16)
    scaled = values * (127.0 / scales.astype(jnp.float32))[..., None]
    codes = jnp.clip(jnp.floor(scaled + 0.5), -127.0, 127.0).astype(jnp.bfloat16)
    return (codes, scales)

def dequantize(codes, scales):
    return (codes.astype(jnp.float32) * (scales.astype(jnp.float32) / 127.0)[..., None]).astype(jnp.bfloat16)

def score_block(query_codes, query_scales, key_codes, key_scales):
    head_size = key_codes.shape[-1]
    factor = 1.0 / (127.0 * 127.0 * math.sqrt(head_size))
    raw = jnp.einsum('thc,uc->htu', query_codes.astype(jnp.float32), key_codes.astype(jnp.float32))
    row_factor = jnp.transpose(query_scales.astype(jnp.float32) * factor)
    return raw * row_factor[:, :, None] * key_scales.astype(jnp.float32)[None, None, :]

def reference(queries, key_rows, value_rows, out_grad, link_mask):
    score_scale = 1.0 / math.sqrt(HD)
    query_float = queries.astype(jnp.float32).reshape(SEQ, HQ, HD)
    query_codes, query_scales = quantize(query_float)
    query_hat = dequantize(query_codes, query_scales)
    key_codes, key_scales = quantize(key_rows.astype(jnp.float32))
    key_hat = dequantize(key_codes, key_scales)
    grad_float = out_grad.astype(jnp.float32).reshape(SEQ, HQ, HD)
    offsets = [0] + [2 ** level for level in range(LEVELS)]
    positions = jnp.arange(TOK_DEV, dtype=jnp.int32)
    causal = (positions[None, :] <= positions[:, None])[None, :, :]

    def one_block(state, block_id):
        key_sum, value_sum = state
        start = (block_id * TOK_DEV).astype(jnp.int32)
        codes_here = lax.dynamic_slice_in_dim(query_codes, start, TOK_DEV, 0)
        scales_here = lax.dynamic_slice_in_dim(query_scales, start, TOK_DEV, 0)
        hat_here = lax.dynamic_slice_in_dim(query_hat, start, TOK_DEV, 0)
        grad_here = lax.dynamic_slice_in_dim(grad_float, start, TOK_DEV, 0)
        score_list = []
        value_list = []
        hat_list = []
        starts = []
        for position, offset in enumerate(offsets):
            source_start = (jnp.maximum(block_id - offset, 0) * TOK_DEV).astype(jnp.int32)
            starts.append(source_start)
            codes_there = lax.dynamic_slice_in_dim(key_codes, source_start, TOK_DEV, 0)
            scales_there = lax.dynamic_slice_in_dim(key_scales, source_start, TOK_DEV, 0)
            value_list.append(lax.dynamic_slice_in_dim(value_rows, source_start, TOK_DEV, 0))
            hat_list.append(lax.dynamic_slice_in_dim(key_hat, source_start, TOK_DEV, 0))
            block_scores = score_block(codes_here, scales_here, codes_there, scales_there)
            if position == 0:
                allowed = causal
            else:
                allowed = jnp.logical_and(block_id >= offset, link_mask[block_id, position - 1] == 1)
            score_list.append(jnp.where(allowed, block_scores, -jnp.inf))
        all_scores = jnp.concatenate(score_list, axis=2)
        values_all = jnp.concatenate(value_list, axis=0)
        hat_all = jnp.concatenate(hat_list, axis=0)
        row_top = lax.optimization_barrier(jnp.max(all_scores, axis=2))
        weights = jnp.exp(all_scores - row_top[:, :, None])
        total = lax.optimization_barrier(jnp.sum(weights, axis=2))
        mixed = jnp.einsum('htu,uc->thc', weights.astype(jnp.bfloat16).astype(jnp.float32), values_all.astype(jnp.float32))
        attended = (mixed / jnp.transpose(total)[:, :, None]).astype(jnp.bfloat16)
        delta = lax.optimization_barrier(jnp.sum(grad_here * attended.astype(jnp.float32), axis=2))
        probs = weights / total[:, :, None]
        grad_probs = jnp.einsum('thc,uc->htu', grad_here, values_all.astype(jnp.float32))
        grad_scores = (probs * (grad_probs - jnp.transpose(delta)[:, :, None]) * score_scale).astype(jnp.bfloat16)
        query_part = jnp.einsum('htu,uc->thc', grad_scores.astype(jnp.float32), hat_all.astype(jnp.float32))
        key_part = jnp.einsum('htu,thc->uc', grad_scores.astype(jnp.float32), hat_here.astype(jnp.float32))
        value_part = jnp.einsum('htu,thc->uc', probs.astype(jnp.bfloat16).astype(jnp.float32), grad_here)
        for position in range(len(offsets)):
            lower = position * TOK_DEV
            old_key = lax.dynamic_slice_in_dim(key_sum, starts[position], TOK_DEV, 0)
            key_sum = lax.dynamic_update_slice_in_dim(key_sum, old_key + key_part[lower:lower + TOK_DEV], starts[position], 0)
            old_value = lax.dynamic_slice_in_dim(value_sum, starts[position], TOK_DEV, 0)
            value_sum = lax.dynamic_update_slice_in_dim(value_sum, old_value + value_part[lower:lower + TOK_DEV], starts[position], 0)
        return ((key_sum, value_sum), (attended.reshape(TOK_DEV, HQ * HD), query_part.astype(jnp.bfloat16).reshape(TOK_DEV, HQ * HD)))
    initial = (jnp.zeros((SEQ, HD), jnp.float32), jnp.zeros((SEQ, HD), jnp.float32))
    (key_sum, value_sum), (attended_all, query_all) = lax.scan(one_block, initial, jnp.arange(BLOCKS, dtype=jnp.int32))
    attention_out = attended_all.reshape(SEQ, HQ * HD)
    query_grad = query_all.reshape(SEQ, HQ * HD)
    return (attention_out, query_grad, key_sum.astype(jnp.bfloat16), value_sum.astype(jnp.bfloat16))
```

```python
import functools
import math

import jax
import jax.numpy as jnp
from jax import lax
from jax.experimental import pallas as pl
from jax.experimental.pallas import tpu as pltpu
from jax.sharding import PartitionSpec as P

scale_eps = 1e-06
MESH = pl.DeviceIdType.MESH
bf16 = jnp.bfloat16
f32 = jnp.float32


def quantize(values):
    largest = jnp.max(jnp.abs(values), axis=1, keepdims=True)
    scales = (largest + scale_eps).astype(bf16).astype(f32)
    codes = jnp.clip(jnp.floor(values * (127.0 / scales) + 0.5), -127.0, 127.0)
    return codes, scales


def dot(left, right):
    return jnp.dot(left, right, preferred_element_type=f32)


def kernel(
    rows, cols, levels, chunk,
    q_ref, k_ref, v_ref, g_ref, link_ref,
    out_ref, dq_ref, dk_ref, dv_ref,
    k_in, v_in, part_out, part_in,
    q_codes_t, q_hat, g_rows, g_aug_t, k_hat_t, v_aug, probs, mixed_t, dq_t, probs_now, ds_now,
    tops, sums, weight_ref,
    send_k, recv_k, send_v, recv_v, send_part, recv_part,
):
    tokens, head = k_ref.shape
    heads = q_ref.shape[1] // head
    width = heads * tokens
    blocks = rows * cols
    block_id = lax.axis_index("row") * cols + lax.axis_index("col")
    score_scale = 1.0 / math.sqrt(head)

    def place(block):
        return (block // cols, lax.rem(block, cols))

    def ahead(distance):
        return place(lax.rem(block_id + distance, blocks))

    def behind(distance):
        return place(lax.rem(block_id + (blocks - distance), blocks))

    barrier = pltpu.get_barrier_semaphore()
    for level in range(levels):
        for partner in (ahead(2**level), behind(2**level)):
            pl.semaphore_signal(barrier, inc=1, device_id=partner, device_id_type=MESH)
    pl.semaphore_wait(barrier, 2 * levels)

    sends = []
    for level in range(levels):
        for source, target, send, recv in (
            (k_ref, k_in, send_k, recv_k),
            (v_ref, v_in, send_v, recv_v),
        ):
            copy = pltpu.make_async_remote_copy(
                src_ref=source,
                dst_ref=target.at[level],
                send_sem=send.at[level],
                recv_sem=recv.at[level],
                device_id=ahead(2**level),
                device_id_type=MESH,
            )
            copy.start()
            sends.append(copy)

    row_factors = []
    for h in range(heads):
        span = pl.ds(h * tokens, tokens)
        codes, scales = quantize(q_ref[:, h * head : (h + 1) * head].astype(f32))
        q_hat[span, :] = (codes * (scales / 127.0)).astype(bf16)
        codes_t = jnp.transpose(codes).astype(bf16)
        q_codes_t[:head, span] = codes_t
        q_codes_t[head:, span] = codes_t
        factor = scales * (1.0 / (127.0 * 127.0 * math.sqrt(head))) * (1.0 / math.log(2.0))
        row_factors.append(jnp.transpose(jnp.broadcast_to(factor, (tokens, head)))[:1, :])
        g_head = g_ref[:, h * head : (h + 1) * head]
        g_rows[span, :] = g_head
        g_aug_t[:head, span] = jnp.transpose(g_head.astype(f32)).astype(bf16)
    row_factor = jnp.concatenate(row_factors, axis=1)
    g_aug_t[head:, :] = jnp.zeros((head, width), bf16)
    v_aug[:, head:] = jnp.ones((tokens, head), bf16)

    def forward(slot, key_rows, values, causal):
        codes, scales = quantize(key_rows[...].astype(f32))
        k_hat_t[slot] = jnp.transpose(codes * (scales / 127.0)).astype(bf16)
        scaled = codes * scales
        high = scaled.astype(bf16)
        low = (scaled - high.astype(f32)).astype(bf16)
        keys = jnp.concatenate([high, low], axis=1)
        values_t = jnp.transpose(values[...].astype(f32)).astype(bf16)
        for start in range(0, width, chunk):
            part = slice(start, start + chunk)
            raw = dot(keys, q_codes_t[:, part])
            if causal:
                key_at = lax.broadcasted_iota(jnp.int32, raw.shape, 0)
                query_at = lax.broadcasted_iota(jnp.int32, raw.shape, 1) + start % tokens
                raw = jnp.where(key_at <= query_at, raw, -jnp.inf)
            factor = row_factor[:, part]
            top = jnp.max(raw, axis=0, keepdims=True) * factor
            weights = jnp.exp2(raw * factor - top)
            tops[slot, :, part] = top
            sums[slot, :, part] = jnp.sum(weights, axis=0, keepdims=True)
            rounded = weights.astype(bf16)
            probs[slot, :, part] = rounded
            mixed_t[slot, :, part] = dot(values_t, rounded)

    forward(levels, k_ref, v_ref, True)

    def forward_level(level, carry):
        for source, target, send, recv in (
            (k_ref, k_in, send_k, recv_k),
            (v_ref, v_in, send_v, recv_v),
        ):
            pltpu.make_async_remote_copy(
                src_ref=source,
                dst_ref=target.at[level],
                send_sem=send.at[level],
                recv_sem=recv.at[level],
                device_id=ahead(1),
                device_id_type=MESH,
            ).wait_recv()
        forward(level, k_in.at[level], v_in.at[level], False)
        return carry

    lax.fori_loop(0, levels, forward_level, 0)

    top_list = [tops[levels]]
    for level in range(levels):
        allowed = jnp.logical_and(block_id >= 2**level, link_ref[0, level] == 1)
        top_list.append(jnp.where(allowed, tops[level], -jnp.inf))
    row_top = functools.reduce(jnp.maximum, top_list)
    shares = [jnp.exp2(top - row_top) for top in top_list]
    slots = [levels] + list(range(levels))
    total = sum(share * sums[slot] for share, slot in zip(shares, slots))
    shares = [share / total for share in shares]
    mixed = sum(share * mixed_t[slot] for share, slot in zip(shares, slots))
    for share, slot in zip(shares, slots):
        weight_ref[slot] = share
    attended_t = mixed.astype(bf16).astype(f32)
    delta = -jnp.sum(g_aug_t[:head, :].astype(f32) * attended_t, axis=0, keepdims=True)
    first = delta.astype(bf16)
    second = (delta - first.astype(f32)).astype(bf16)
    third = (delta - first.astype(f32) - second.astype(f32)).astype(bf16)
    row_at = lax.broadcasted_iota(jnp.int32, (16, width), 0)
    g_aug_t[head : head + 16, :] = jnp.where(
        row_at == 0,
        first.astype(f32),
        jnp.where(
            row_at == 1, second.astype(f32), jnp.where(row_at == 2, third.astype(f32), 0.0)
        ),
    ).astype(bf16)
    for h in range(heads):
        out_ref[:, h * head : (h + 1) * head] = jnp.transpose(
            attended_t[:, h * tokens : (h + 1) * tokens]
        ).astype(bf16)
    dq_t[...] = jnp.zeros_like(dq_t)

    def backward(slot, values):
        v_aug[:, :head] = values[...]
        for start in range(0, width, chunk):
            part = slice(start, start + chunk)
            share = weight_ref[slot, :, part].astype(bf16)
            prob = probs[slot, :, part] * share
            grad = dot(v_aug[...], g_aug_t[:, part]).astype(bf16) * prob
            probs_now[:, part] = prob
            ds_now[:, part] = grad
            dq_t[:, part] += dot(k_hat_t[slot], grad)
        return dot(ds_now[...], q_hat[...]) * score_scale, dot(probs_now[...], g_rows[...])

    def part_copy(level, kind, device):
        return pltpu.make_async_remote_copy(
            src_ref=part_out.at[level, kind],
            dst_ref=part_in.at[level, kind],
            send_sem=send_part.at[level, kind],
            recv_sem=recv_part.at[level, kind],
            device_id=device,
            device_id_type=MESH,
        )

    def backward_level(level, distance):
        key_part, value_part = backward(level, v_in.at[level])
        part_out[level, 0] = key_part.astype(bf16)
        part_out[level, 1] = value_part.astype(bf16)
        for kind in range(2):
            part_copy(level, kind, behind(distance)).start()
        return distance * 2

    lax.fori_loop(0, levels, backward_level, jnp.int32(1))
    key_sum, value_sum = backward(levels, v_ref)
    for h in range(heads):
        dq_ref[:, h * head : (h + 1) * head] = (
            jnp.transpose(dq_t[:, h * tokens : (h + 1) * tokens]) * score_scale
        ).astype(bf16)
    for level in range(levels):
        for kind in range(2):
            part_copy(level, kind, behind(2**level)).wait_recv()
        key_sum = key_sum + part_in[level, 0].astype(f32)
        value_sum = value_sum + part_in[level, 1].astype(f32)
    dk_ref[...] = key_sum.astype(bf16)
    dv_ref[...] = value_sum.astype(bf16)
    for copy in sends:
        copy.wait_send()
    for level in range(levels):
        for kind in range(2):
            part_copy(level, kind, behind(2**level)).wait_send()


def local(rows, cols, queries, key_rows, value_rows, out_grad, link_mask):
    tokens, head = key_rows.shape
    heads = queries.shape[1] // head
    levels = link_mask.shape[1]
    width = heads * tokens
    sources = levels + 1
    dma = pltpu.SemaphoreType.DMA
    vmem = pl.BlockSpec(memory_space=pltpu.VMEM)
    return pl.pallas_call(
        functools.partial(kernel, rows, cols, levels, min(256, tokens)),
        out_shape=(
            jax.ShapeDtypeStruct(queries.shape, bf16),
            jax.ShapeDtypeStruct(queries.shape, bf16),
            jax.ShapeDtypeStruct(key_rows.shape, bf16),
            jax.ShapeDtypeStruct(value_rows.shape, bf16),
        ),
        in_specs=[vmem, vmem, vmem, vmem, pl.BlockSpec(memory_space=pltpu.SMEM)],
        out_specs=(vmem, vmem, vmem, vmem),
        scratch_shapes=[
            pltpu.VMEM((levels, tokens, head), bf16),
            pltpu.VMEM((levels, tokens, head), bf16),
            pltpu.VMEM((levels, 2, tokens, head), bf16),
            pltpu.VMEM((levels, 2, tokens, head), bf16),
            pltpu.VMEM((2 * head, width), bf16),
            pltpu.VMEM((width, head), bf16),
            pltpu.VMEM((width, head), bf16),
            pltpu.VMEM((2 * head, width), bf16),
            pltpu.VMEM((sources, head, tokens), bf16),
            pltpu.VMEM((tokens, 2 * head), bf16),
            pltpu.VMEM((sources, tokens, width), bf16),
            pltpu.VMEM((sources, head, width), f32),
            pltpu.VMEM((head, width), f32),
            pltpu.VMEM((tokens, width), bf16),
            pltpu.VMEM((tokens, width), bf16),
            pltpu.VMEM((sources, 1, width), f32),
            pltpu.VMEM((sources, 1, width), f32),
            pltpu.VMEM((sources, 1, width), f32),
            dma((levels,)),
            dma((levels,)),
            dma((levels,)),
            dma((levels,)),
            dma((levels, 2)),
            dma((levels, 2)),
        ],
        compiler_params=pltpu.CompilerParams(
            collective_id=0, has_side_effects=True, vmem_limit_bytes=48 * 2**20
        ),
    )(queries, key_rows, value_rows, out_grad, link_mask)


def solution(mesh):
    spec = P(("row", "col"), None)
    return jax.shard_map(
        functools.partial(local, mesh.shape["row"], mesh.shape["col"]),
        mesh=mesh,
        in_specs=(spec,) * 5,
        out_specs=(spec,) * 4,
        check_vma=False,
    )
```

```python
import functools
import math

import jax
import jax.numpy as jnp
from jax import lax
from jax.experimental import pallas as pl
from jax.experimental.pallas import tpu as pltpu
from jax.sharding import PartitionSpec as P

scale_eps = 1e-06
MESH = pl.DeviceIdType.MESH
bf16 = jnp.bfloat16
f32 = jnp.float32
RING = 4
NEAR, TWO, GROUP, PAIR, FAR = range(5)
KEY, VALUE = 0, 1


def quantize(values):
    largest = jnp.max(jnp.abs(values), axis=1, keepdims=True)
    scales = (largest + scale_eps).astype(bf16).astype(f32)
    codes = jnp.clip(jnp.floor(values * (127.0 / scales) + 0.5), -127.0, 127.0)
    return codes, scales


def dot(left, right):
    return jnp.dot(left, right, preferred_element_type=f32)


def kernel(
    rows, cols, levels, chunk,
    q_hbm, k_hbm, v_hbm, g_hbm, link_ref,
    out_ref, dq_ref, dk_ref, dv_ref,
    q_ref, g_ref, kv, kv_in, part_out, part_in, held,
    keys, q_codes_t, q_hat, g_rows, g_aug_t, k_hat_t, values_t, scores, probs, ds, tops,
    load_sem, send_fwd, recv_fwd, send_bwd, recv_bwd,
):
    tokens, head = k_hbm.shape
    heads = q_hbm.shape[1] // head
    width = heads * tokens
    blocks = rows * cols
    block_id = lax.axis_index("row") * cols + lax.axis_index("col")
    score_scale = 1.0 / math.sqrt(head)
    in_ring = lax.rem(block_id, RING)
    ring_start = block_id - in_ring
    core = lax.rem(block_id // 8, 2)
    distances = [2**level for level in range(levels)]

    def place(block):
        return (block // cols, lax.rem(block, cols))

    def ring(steps):
        return ring_start + lax.rem(in_ring + steps, RING)

    partner = block_id + 8 - 16 * core
    ahead = [ring(1), ring(2), block_id + 4, partner, block_id + 16]
    behind = [ring(3), ring(2), block_id - 4, partner, block_id - 16]

    loads = []
    for index, (source, target) in enumerate(
        ((k_hbm, kv.at[KEY]), (v_hbm, kv.at[VALUE]), (q_hbm, q_ref), (g_hbm, g_ref))
    ):
        copy = pltpu.make_async_copy(source, target, load_sem.at[index])
        copy.start()
        loads.append(copy)

    def has_next(level):
        return block_id + distances[level] < blocks

    def has_prev(level):
        return block_id >= distances[level]

    barrier = pltpu.get_barrier_semaphore()

    def greet(block):
        pl.semaphore_signal(barrier, inc=1, device_id=place(block), device_id_type=MESH)

    for other in (ring(1), ring(2), ring(3), partner):
        greet(other)
    for level in (GROUP, FAR):
        pl.when(has_next(level))(functools.partial(greet, ahead[level]))
        pl.when(has_prev(level))(functools.partial(greet, behind[level]))

    for level in range(GROUP, levels):
        @pl.when(jnp.logical_not(has_prev(level)))
        def _():
            kv_in[level] = jnp.zeros(kv_in.shape[1:], bf16)

    for level in (GROUP, FAR):
        @pl.when(jnp.logical_not(has_next(level)))
        def _():
            part_in[level] = jnp.zeros(part_in.shape[1:], bf16)

    met = sum(has(level).astype(jnp.int32) for level in (GROUP, FAR) for has in (has_next, has_prev))
    for copy in loads[:2]:
        copy.wait()
    pl.semaphore_wait(barrier, 4 + met)

    def forward_copy(level, kind, source):
        return pltpu.make_async_remote_copy(
            src_ref=source.at[kind],
            dst_ref=kv_in.at[level, kind],
            send_sem=send_fwd.at[level, kind],
            recv_sem=recv_fwd.at[level, kind],
            device_id=place(ahead[level]),
            device_id_type=MESH,
        )

    def send_rows(condition, level, kind, source):
        @pl.when(condition)
        def _():
            forward_copy(level, kind, source).start()

    def wait_rows(level, kind):
        if level < GROUP:
            forward_copy(level, kind, kv).wait_recv()
        else:
            @pl.when(has_prev(level))
            def _():
                forward_copy(level, kind, kv).wait_recv()

    relays_pair = jnp.logical_and(core == 1, has_prev(FAR))
    for kind in (KEY, VALUE):
        send_rows(has_next(FAR), FAR, kind, kv)
        send_rows(has_next(GROUP), GROUP, kind, kv)
        send_rows(core == 0, PAIR, kind, kv)
        send_rows(in_ring < RING - 1, NEAR, kind, kv)
        send_rows(in_ring < RING - 2, TWO, kind, kv)

    def pass_far(kind):
        wait_rows(FAR, kind)
        send_rows(relays_pair, PAIR, kind, kv_in.at[FAR])

    def pass_group(kind):
        wait_rows(GROUP, kind)
        send_rows(in_ring >= RING - 1, NEAR, kind, kv_in.at[GROUP])
        send_rows(in_ring >= RING - 2, TWO, kind, kv_in.at[GROUP])

    for copy in loads[2:]:
        copy.wait()
    row_factors = []
    for h in range(heads):
        span = pl.ds(h * tokens, tokens)
        codes, scales = quantize(q_ref[:, h * head : (h + 1) * head].astype(f32))
        q_hat[span, :] = (codes * (scales / 127.0)).astype(bf16)
        codes_t = jnp.transpose(codes.astype(bf16))
        q_codes_t[:head, span] = codes_t
        q_codes_t[head:, span] = codes_t
        factor = scales * (1.0 / (127.0 * 127.0 * math.sqrt(head))) * (1.0 / math.log(2.0))
        row_factors.append(jnp.transpose(jnp.broadcast_to(factor, (tokens, head)))[:1, :])
        g_head = g_ref[:, h * head : (h + 1) * head]
        g_aug_t[:head, span] = jnp.transpose(g_head)
    row_factor = jnp.concatenate(row_factors, axis=1)
    g_aug_t[head:, :] = jnp.zeros((head, width), bf16)

    def rows_of(slot):
        return kv if slot == levels else kv_in.at[slot]

    def fold(values, reduce):
        return reduce(values.reshape(-1, 8, values.shape[1]), axis=0)

    parts = [slice(start, start + chunk) for start in range(0, width, chunk)]

    def score(slot):
        codes, scales = quantize(rows_of(slot)[KEY].astype(f32))
        span = slice(slot * tokens, (slot + 1) * tokens)
        k_hat_t[:, span] = jnp.transpose((codes * (scales / 127.0)).astype(bf16))
        scaled = codes * scales
        high = scaled.astype(bf16)
        keys[:, :head] = high
        keys[:, head:] = (scaled - high.astype(f32)).astype(bf16)
        for part in parts:
            raw = dot(keys[...], q_codes_t[:, part])
            if slot == levels:
                key_at = lax.broadcasted_iota(jnp.int32, raw.shape, 0)
                query_at = lax.broadcasted_iota(jnp.int32, raw.shape, 1) + part.start % tokens
                raw = jnp.where(key_at <= query_at, raw, -jnp.inf)
            scores[span, part] = raw
            tops[slot, :, part] = fold(raw, jnp.max)

    pass_far(KEY)
    score(levels)
    pass_group(KEY)
    score(FAR)
    pass_far(VALUE)
    score(GROUP)
    pass_group(VALUE)
    for slot in (PAIR, NEAR, TWO):
        wait_rows(slot, KEY)
        score(slot)
    for slot in (PAIR, NEAR, TWO):
        wait_rows(slot, VALUE)
    order = (PAIR, TWO, NEAR, FAR, GROUP, levels)

    allowed = [
        jnp.logical_and(has_prev(level), link_ref[0, level] == 1) for level in range(levels)
    ]
    level_tops = [jnp.max(tops[slot], axis=0, keepdims=True) for slot in range(levels + 1)]
    row_top = level_tops[levels]
    for level in range(levels):
        row_top = jnp.maximum(row_top, jnp.where(allowed[level], level_tops[level], -jnp.inf))
    row_top = row_top * row_factor

    total = jnp.zeros((8, width), f32)
    tile = 128
    for slot in order:
        factor, top = row_factor, row_top
        if slot < levels:
            factor = jnp.where(allowed[slot], factor, 0.0)
            top = jnp.where(allowed[slot], top, 1e30)
        values_t[:, slot * tokens : (slot + 1) * tokens] = jnp.transpose(rows_of(slot)[VALUE])
        sums = []
        for part in parts:
            acc = jnp.zeros((8, chunk), f32)
            for start in range(slot * tokens, (slot + 1) * tokens, tile):
                span = slice(start, start + tile)
                weights = jnp.exp2(scores[span, part] * factor[:, part] - top[:, part])
                acc = acc + fold(weights, jnp.sum)
                probs[span, part] = weights.astype(bf16)
            sums.append(acc)
        total = total + jnp.concatenate(sums, axis=1)
    scale_row = 1.0 / jnp.sum(total, axis=0, keepdims=True)
    scale_column = jnp.transpose(jnp.broadcast_to(scale_row, (head, width)))
    for h in range(heads):
        span = slice(h * tokens, (h + 1) * tokens)
        g_head = g_ref[:, h * head : (h + 1) * head].astype(f32)
        g_rows[span, :] = (g_head * scale_column[span]).astype(bf16)
    q_hat[...] = (q_hat[...].astype(f32) * (scale_column * score_scale)).astype(bf16)

    def back_copy(level, kind):
        return pltpu.make_async_remote_copy(
            src_ref=part_out.at[level, kind],
            dst_ref=part_in.at[level, kind],
            send_sem=send_bwd.at[level, kind],
            recv_sem=recv_bwd.at[level, kind],
            device_id=place(behind[level]),
            device_id_type=MESH,
        )

    def wait_part(level, kind):
        if level in (GROUP, FAR):
            @pl.when(has_next(level))
            def _():
                back_copy(level, kind).wait_recv()
        else:
            back_copy(level, kind).wait_recv()

    def chosen(condition, level, kind):
        return jnp.where(condition, part_in[level, kind].astype(f32), 0.0)

    group_sends_now = jnp.logical_and(has_prev(GROUP), in_ring < RING - 2)
    group_relays = jnp.logical_and(has_prev(GROUP), in_ring >= RING - 2)

    def give(level, kind, part):
        if level == FAR:
            wait_part(PAIR, kind)
            part = part + chosen(core == 1, PAIR, kind)
        if level == GROUP:
            held[kind] = part
        part_out[level, kind] = part.astype(bf16)
        if level in (NEAR, TWO, PAIR):
            back_copy(level, kind).start()
        else:
            @pl.when(has_prev(FAR) if level == FAR else group_sends_now)
            def _():
                back_copy(level, kind).start()

    def relay(kind):
        wait_part(NEAR, kind)
        wait_part(TWO, kind)

        @pl.when(group_relays)
        def _():
            part = held[kind] + chosen(in_ring == RING - 1, NEAR, kind) + part_in[TWO, kind].astype(f32)
            part_out[GROUP, kind] = part.astype(bf16)
            back_copy(GROUP, kind).start()

    own = [None, None]

    def all_rows(slot):
        return slice(slot * tokens, (slot + 1) * tokens)

    for slot in order:
        part = dot(probs[all_rows(slot), :], g_rows[...])
        if slot == levels:
            own[VALUE] = part
        else:
            give(slot, VALUE, part)

    attended = []
    for part in parts:
        mixed = dot(values_t[...], probs[:, part])
        attended_t = (mixed * scale_row[:, part]).astype(bf16)
        attended.append(attended_t)
        delta = -jnp.sum(
            g_aug_t[:head, part].astype(f32) * attended_t.astype(f32), axis=0, keepdims=True
        )
        first = delta.astype(bf16).astype(f32)
        second = (delta - first).astype(bf16).astype(f32)
        third = delta - first - second
        row_at = lax.broadcasted_iota(jnp.int32, (16, chunk), 0)
        pieces = jnp.where(row_at == 0, first, jnp.where(row_at == 1, second, third))
        g_aug_t[head : head + 16, part] = jnp.where(row_at < 3, pieces, 0.0).astype(bf16)

    ones = jnp.ones((tokens, head), bf16)
    for slot in order:
        v_aug = jnp.concatenate([rows_of(slot)[VALUE], ones], axis=1)
        for part in parts:
            grad = dot(v_aug, g_aug_t[:, part]).astype(bf16)
            ds[all_rows(slot), part] = grad * probs[all_rows(slot), part]
        part = dot(ds[all_rows(slot), :], q_hat[...])
        if slot == levels:
            own[KEY] = part
        else:
            give(slot, KEY, part)

    relay(VALUE)
    per_head = tokens // chunk
    for index, part in enumerate(parts):
        h = index // per_head
        rows_here = slice(part.start - h * tokens, part.stop - h * tokens)
        columns = slice(h * head, (h + 1) * head)
        grad_t = dot(k_hat_t[...], ds[:, part]) * (scale_row[:, part] * score_scale)
        dq_ref[rows_here, columns] = jnp.transpose(grad_t.astype(bf16))
        out_ref[rows_here, columns] = jnp.transpose(attended[index])
    relay(KEY)

    for kind, target in ((VALUE, dv_ref), (KEY, dk_ref)):
        for level in (GROUP, FAR):
            wait_part(level, kind)
        total_part = own[kind]
        for level, mine in (
            (NEAR, in_ring < RING - 1), (TWO, in_ring < RING - 2), (GROUP, has_next(GROUP)),
            (PAIR, core == 0), (FAR, has_next(FAR)),
        ):
            total_part = total_part + chosen(mine, level, kind)
        target[...] = total_part.astype(bf16)
    for kind in (KEY, VALUE):
        for level in range(levels):
            sent = {
                NEAR: True, TWO: True, GROUP: has_next(GROUP), FAR: has_next(FAR),
                PAIR: jnp.logical_or(core == 0, relays_pair),
            }[level]
            back = {NEAR: True, TWO: True, PAIR: True}.get(level, has_prev(level))
            for condition, copy in (
                (sent, forward_copy(level, kind, kv)), (back, back_copy(level, kind))
            ):
                if condition is True:
                    copy.wait_send()
                else:
                    pl.when(condition)(copy.wait_send)


def local(rows, cols, queries, key_rows, value_rows, out_grad, link_mask):
    tokens, head = key_rows.shape
    heads = queries.shape[1] // head
    levels = link_mask.shape[1]
    width = heads * tokens
    sources = levels + 1
    dma = pltpu.SemaphoreType.DMA
    vmem = pl.BlockSpec(memory_space=pltpu.VMEM)
    hbm = pl.BlockSpec(memory_space=pl.ANY)
    return pl.pallas_call(
        functools.partial(kernel, rows, cols, levels, min(256, tokens)),
        out_shape=(
            jax.ShapeDtypeStruct(queries.shape, bf16),
            jax.ShapeDtypeStruct(queries.shape, bf16),
            jax.ShapeDtypeStruct(key_rows.shape, bf16),
            jax.ShapeDtypeStruct(value_rows.shape, bf16),
        ),
        in_specs=[hbm, hbm, hbm, hbm, pl.BlockSpec(memory_space=pltpu.SMEM)],
        out_specs=(vmem, vmem, vmem, vmem),
        scratch_shapes=[
            pltpu.VMEM(queries.shape, bf16),
            pltpu.VMEM(queries.shape, bf16),
            pltpu.VMEM((2, tokens, head), bf16),
            pltpu.VMEM((levels, 2, tokens, head), bf16),
            pltpu.VMEM((levels, 2, tokens, head), bf16),
            pltpu.VMEM((levels, 2, tokens, head), bf16),
            pltpu.VMEM((2, tokens, head), f32),
            pltpu.VMEM((tokens, 2 * head), bf16),
            pltpu.VMEM((2 * head, width), bf16),
            pltpu.VMEM((width, head), bf16),
            pltpu.VMEM((width, head), bf16),
            pltpu.VMEM((2 * head, width), bf16),
            pltpu.VMEM((head, sources * tokens), bf16),
            pltpu.VMEM((head, sources * tokens), bf16),
            pltpu.VMEM((sources * tokens, width), f32),
            pltpu.VMEM((sources * tokens, width), bf16),
            pltpu.VMEM((sources * tokens, width), bf16),
            pltpu.VMEM((sources, 8, width), f32),
            dma((4,)),
            dma((levels, 2)),
            dma((levels, 2)),
            dma((levels, 2)),
            dma((levels, 2)),
        ],
        compiler_params=pltpu.CompilerParams(
            collective_id=0, has_side_effects=True, vmem_limit_bytes=60 * 2**20
        ),
    )(queries, key_rows, value_rows, out_grad, link_mask)


def solution(mesh):
    spec = P(("row", "col"), None)
    return jax.shard_map(
        functools.partial(local, mesh.shape["row"], mesh.shape["col"]),
        mesh=mesh,
        in_specs=(spec,) * 5,
        out_specs=(spec,) * 4,
        check_vma=False,
    )
```

```python
import functools
import math

import jax
import jax.numpy as jnp
from jax import lax
from jax.experimental import pallas as pl
from jax.experimental.pallas import tpu as pltpu
from jax.sharding import PartitionSpec as P

scale_eps = 1e-06
MESH = pl.DeviceIdType.MESH
bf16 = jnp.bfloat16
f32 = jnp.float32
RING = 4
NEAR, TWO, GROUP, PAIR, FAR = range(5)
KEY, VALUE = 0, 1
HALVES = 2


def quantize(values):
    largest = jnp.max(jnp.abs(values), axis=1, keepdims=True)
    scales = (largest + scale_eps).astype(bf16).astype(f32)
    codes = jnp.clip(jnp.floor(values * (127.0 / scales) + 0.5), -127.0, 127.0)
    return codes, scales


def dot(left, right):
    return jnp.dot(left, right, preferred_element_type=f32)


def kernel(
    rows, cols, levels, chunk,
    q_hbm, k_hbm, v_hbm, g_hbm, link_ref,
    out_ref, dq_ref, dk_ref, dv_ref,
    q_ref, g_ref, kv, kv_in, via, part_out, part_in, held,
    keys, q_codes_t, q_hat, g_rows, g_aug_t, k_hat_t, values_t, scores, probs, ds, tops,
    load_sem, send_fwd, recv_fwd, send_via, recv_via, send_hop, send_bwd, recv_bwd,
):
    tokens, head = k_hbm.shape
    heads = q_hbm.shape[1] // head
    width = heads * tokens
    blocks = rows * cols
    block_id = lax.axis_index("row") * cols + lax.axis_index("col")
    score_scale = 1.0 / math.sqrt(head)
    in_ring = lax.rem(block_id, RING)
    ring_start = block_id - in_ring
    core = lax.rem(block_id // 8, 2)
    distances = [2**level for level in range(levels)]

    def place(block):
        return (block // cols, lax.rem(block, cols))

    def ring(steps):
        return ring_start + lax.rem(in_ring + steps, RING)

    partner = block_id + 8 - 16 * core
    ahead = [ring(1), ring(2), block_id + 4, partner, block_id + 16]
    behind = [ring(3), ring(2), block_id - 4, partner, block_id - 16]

    loads = []
    for index, (source, target) in enumerate(
        ((k_hbm, kv.at[KEY]), (v_hbm, kv.at[VALUE]), (q_hbm, q_ref), (g_hbm, g_ref))
    ):
        copy = pltpu.make_async_copy(source, target, load_sem.at[index])
        copy.start()
        loads.append(copy)

    def has_next(level):
        return block_id + distances[level] < blocks

    def has_prev(level):
        return block_id >= distances[level]

    barrier = pltpu.get_barrier_semaphore()

    def greet(block):
        pl.semaphore_signal(barrier, inc=1, device_id=place(block), device_id_type=MESH)

    for other in (ring(1), ring(2), ring(3), partner):
        greet(other)
    for level in (GROUP, FAR):
        pl.when(has_next(level))(functools.partial(greet, ahead[level]))
        pl.when(has_prev(level))(functools.partial(greet, behind[level]))

    for level in range(GROUP, levels):
        @pl.when(jnp.logical_not(has_prev(level)))
        def _():
            kv_in[level] = jnp.zeros(kv_in.shape[1:], bf16)

    for level in (GROUP, FAR):
        @pl.when(jnp.logical_not(has_next(level)))
        def _():
            part_in[level] = jnp.zeros(part_in.shape[1:], bf16)

    met = sum(has(level).astype(jnp.int32) for level in (GROUP, FAR) for has in (has_next, has_prev))
    for copy in loads[:2]:
        copy.wait()
    pl.semaphore_wait(barrier, 4 + met)

    half = tokens // HALVES
    pieces = [(kind, piece) for kind in (KEY, VALUE) for piece in range(HALVES)]

    def forward_copy(level, kind, piece, source):
        span = pl.ds(piece * half, half)
        return pltpu.make_async_remote_copy(
            src_ref=source.at[kind, span],
            dst_ref=kv_in.at[level, kind, span],
            send_sem=send_fwd.at[level, kind, piece],
            recv_sem=recv_fwd.at[level, kind, piece],
            device_id=place(ahead[level]),
            device_id_type=MESH,
        )

    def hop_copy(kind, piece, source, steps, sent):
        span = pl.ds(piece * half, half)
        return pltpu.make_async_remote_copy(
            src_ref=source.at[span],
            dst_ref=kv_in.at[TWO, kind, span],
            send_sem=sent,
            recv_sem=recv_fwd.at[TWO, kind, piece],
            device_id=place(ring(steps)),
            device_id_type=MESH,
        )

    def near_copy(piece):
        return hop_copy(KEY, piece, kv_in.at[NEAR, KEY], 1, send_fwd.at[TWO, KEY, piece])

    def last_copy(kind, piece):
        return hop_copy(kind, piece, via.at[kind], RING - 1, send_hop.at[kind, piece])

    def via_copy(kind, piece, source):
        span = pl.ds(piece * half, half)
        return pltpu.make_async_remote_copy(
            src_ref=source.at[kind, span],
            dst_ref=via.at[kind, span],
            send_sem=send_via.at[kind, piece],
            recv_sem=recv_via.at[kind, piece],
            device_id=place(ring(RING - 1)),
            device_id_type=MESH,
        )

    def pass_near(condition, piece):
        @pl.when(condition)
        def _():
            wait_rows(NEAR, KEY, piece)

        @pl.when(jnp.logical_and(condition, in_ring < RING - 1))
        def _():
            near_copy(piece).start()

    def pass_via(kind, piece):
        @pl.when(in_ring == 1 if kind == KEY else in_ring >= 0)
        def _():
            via_copy(kind, piece, kv).wait_recv()
            last_copy(kind, piece).start()

    def send_rows(condition, level, kind, piece, source):
        @pl.when(condition)
        def _():
            forward_copy(level, kind, piece, source).start()

    def wait_rows(level, kind, piece):
        if level < GROUP:
            forward_copy(level, kind, piece, kv).wait_recv()
        else:
            @pl.when(has_prev(level))
            def _():
                forward_copy(level, kind, piece, kv).wait_recv()

    relays_pair = jnp.logical_and(core == 1, has_prev(FAR))
    for kind, piece in pieces:
        send_rows(has_next(GROUP), GROUP, kind, piece, kv)
        send_rows(has_next(FAR), FAR, kind, piece, kv)
        if kind == VALUE:
            pl.when(in_ring < RING - 2)(via_copy(kind, piece, kv).start)
        send_rows(in_ring < RING - 1, NEAR, kind, piece, kv)
        send_rows(core == 0, PAIR, kind, piece, kv)

    def pass_far(kind, piece):
        wait_rows(FAR, kind, piece)
        send_rows(relays_pair, PAIR, kind, piece, kv_in.at[FAR])

    def pass_group(kind, piece):
        wait_rows(GROUP, kind, piece)
        send_rows(in_ring >= RING - 1, NEAR, kind, piece, kv_in.at[GROUP])
        late = in_ring == RING - 2 if kind == KEY else in_ring >= RING - 2
        pl.when(late)(via_copy(kind, piece, kv_in.at[GROUP]).start)

    for copy in loads[2:]:
        copy.wait()
    row_factors = []
    for h in range(heads):
        span = pl.ds(h * tokens, tokens)
        codes, scales = quantize(q_ref[:, h * head : (h + 1) * head].astype(f32))
        q_hat[span, :] = (codes * (scales / 127.0)).astype(bf16)
        codes_t = jnp.transpose(codes.astype(bf16))
        q_codes_t[:head, span] = codes_t
        q_codes_t[head:, span] = codes_t
        factor = scales * (1.0 / (127.0 * 127.0 * math.sqrt(head))) * (1.0 / math.log(2.0))
        row_factors.append(jnp.transpose(jnp.broadcast_to(factor, (tokens, head)))[:1, :])
        g_head = g_ref[:, h * head : (h + 1) * head]
        g_aug_t[:head, span] = jnp.transpose(g_head)
    row_factor = jnp.concatenate(row_factors, axis=1)
    g_aug_t[head:, :] = jnp.zeros((head, width), bf16)

    def rows_of(slot):
        return kv if slot == levels else kv_in.at[slot]

    def fold(values, reduce):
        return reduce(values.reshape(-1, 8, values.shape[1]), axis=0)

    def all_rows(slot):
        return slice(slot * tokens, (slot + 1) * tokens)

    parts = [slice(start, start + chunk) for start in range(0, width, chunk)]

    def score(slot):
        codes, scales = quantize(rows_of(slot)[KEY].astype(f32))
        span = slice(slot * tokens, (slot + 1) * tokens)
        k_hat_t[:, span] = jnp.transpose((codes * (scales / 127.0)).astype(bf16))
        scaled = codes * scales
        high = scaled.astype(bf16)
        keys[:, :head] = high
        keys[:, head:] = (scaled - high.astype(f32)).astype(bf16)
        for part in parts:
            raw = dot(keys[...], q_codes_t[:, part])
            if slot == levels:
                key_at = lax.broadcasted_iota(jnp.int32, raw.shape, 0)
                query_at = lax.broadcasted_iota(jnp.int32, raw.shape, 1) + part.start % tokens
                raw = jnp.where(key_at <= query_at, raw, -jnp.inf)
            scores[span, part] = raw
            tops[slot, :, part] = fold(raw, jnp.max)

    score(levels)
    early = jnp.logical_or(in_ring == 1, in_ring == 2)
    for piece in range(HALVES):
        pass_near(early, piece)
    for piece in range(HALVES):
        pass_group(KEY, piece)
        pass_far(KEY, piece)
    score(GROUP)
    for piece in range(HALVES):
        pass_near(jnp.logical_not(early), piece)
        pass_via(KEY, piece)
    pass_group(VALUE, 0)
    pass_far(VALUE, 0)
    score(FAR)
    pass_group(VALUE, 1)
    pass_far(VALUE, 1)
    score(NEAR)
    pass_via(VALUE, 0)
    for piece in range(HALVES):
        wait_rows(PAIR, KEY, piece)
    score(PAIR)
    pass_via(VALUE, 1)
    for piece in range(HALVES):
        wait_rows(TWO, KEY, piece)
    score(TWO)
    order = (PAIR, TWO, NEAR, FAR, GROUP, levels)

    allowed = [
        jnp.logical_and(has_prev(level), link_ref[0, level] == 1) for level in range(levels)
    ]
    level_tops = [jnp.max(tops[slot], axis=0, keepdims=True) for slot in range(levels + 1)]
    row_top = level_tops[levels]
    for level in range(levels):
        row_top = jnp.maximum(row_top, jnp.where(allowed[level], level_tops[level], -jnp.inf))
    row_top = row_top * row_factor

    total = jnp.zeros((8, width), f32)
    tile = 128
    for slot in order:
        factor, top = row_factor, row_top
        if slot < levels:
            factor = jnp.where(allowed[slot], factor, 0.0)
            top = jnp.where(allowed[slot], top, 1e30)
        sums = []
        for part in parts:
            acc = jnp.zeros((8, chunk), f32)
            for start in range(slot * tokens, (slot + 1) * tokens, tile):
                span = slice(start, start + tile)
                weights = jnp.exp2(scores[span, part] * factor[:, part] - top[:, part])
                acc = acc + fold(weights, jnp.sum)
                probs[span, part] = weights.astype(bf16)
            sums.append(acc)
        total = total + jnp.concatenate(sums, axis=1)
    scale_row = 1.0 / jnp.sum(total, axis=0, keepdims=True)
    scale_column = jnp.transpose(jnp.broadcast_to(scale_row, (head, width)))
    for h in range(heads):
        span = slice(h * tokens, (h + 1) * tokens)
        g_head = g_ref[:, h * head : (h + 1) * head].astype(f32)
        g_rows[span, :] = (g_head * scale_column[span]).astype(bf16)
    q_hat[...] = (q_hat[...].astype(f32) * (scale_column * score_scale)).astype(bf16)

    def back_copy(level, kind, piece):
        span = pl.ds(piece * half, half)
        return pltpu.make_async_remote_copy(
            src_ref=part_out.at[level, kind, span],
            dst_ref=part_in.at[level, kind, span],
            send_sem=send_bwd.at[level, kind, piece],
            recv_sem=recv_bwd.at[level, kind, piece],
            device_id=place(behind[level]),
            device_id_type=MESH,
        )

    def wait_part(level, kind, piece):
        if level in (GROUP, FAR):
            @pl.when(has_next(level))
            def _():
                back_copy(level, kind, piece).wait_recv()
        else:
            back_copy(level, kind, piece).wait_recv()

    def chosen(condition, level, kind, span=slice(None)):
        return jnp.where(condition, part_in[level, kind, span].astype(f32), 0.0)

    group_sends_now = jnp.logical_and(has_prev(GROUP), in_ring < RING - 2)
    group_relays = jnp.logical_and(has_prev(GROUP), in_ring >= RING - 2)
    spans = [slice(piece * half, (piece + 1) * half) for piece in range(HALVES)]

    def give(level, kind, part):
        if level == GROUP:
            held[kind] = part
        for piece, span in enumerate(spans):
            here = part[span]
            if level == FAR:
                wait_part(PAIR, kind, piece)
                here = here + chosen(core == 1, PAIR, kind, span)
            part_out[level, kind, span] = here.astype(bf16)
            if level in (NEAR, TWO, PAIR):
                back_copy(level, kind, piece).start()
            else:
                @pl.when(has_prev(FAR) if level == FAR else group_sends_now)
                def _():
                    back_copy(level, kind, piece).start()

    def relay(kind):
        for piece, span in enumerate(spans):
            wait_part(TWO, kind, piece)
            wait_part(NEAR, kind, piece)

            @pl.when(group_relays)
            def _():
                part = held[kind, span] + part_in[TWO, kind, span].astype(f32)
                part = part + chosen(in_ring == RING - 1, NEAR, kind, span)
                part_out[GROUP, kind, span] = part.astype(bf16)
                back_copy(GROUP, kind, piece).start()

    own = [None, None]

    for slot in order:
        part = dot(probs[all_rows(slot), :], g_rows[...])
        if slot == levels:
            own[VALUE] = part
        else:
            give(slot, VALUE, part)

    for slot in (PAIR, NEAR, TWO):
        for piece in range(HALVES):
            wait_rows(slot, VALUE, piece)
    for slot in order:
        values_t[:, all_rows(slot)] = jnp.transpose(rows_of(slot)[VALUE])

    attended = []
    for part in parts:
        mixed = dot(values_t[...], probs[:, part])
        attended_t = (mixed * scale_row[:, part]).astype(bf16)
        attended.append(attended_t)
        delta = -jnp.sum(
            g_aug_t[:head, part].astype(f32) * attended_t.astype(f32), axis=0, keepdims=True
        )
        first = delta.astype(bf16).astype(f32)
        second = (delta - first).astype(bf16).astype(f32)
        third = delta - first - second
        row_at = lax.broadcasted_iota(jnp.int32, (16, chunk), 0)
        split = jnp.where(row_at == 0, first, jnp.where(row_at == 1, second, third))
        g_aug_t[head : head + 16, part] = jnp.where(row_at < 3, split, 0.0).astype(bf16)

    ones = jnp.ones((tokens, head), bf16)
    for slot in order:
        if slot == FAR:
            relay(VALUE)
        v_aug = jnp.concatenate([rows_of(slot)[VALUE], ones], axis=1)
        for part in parts:
            grad = dot(v_aug, g_aug_t[:, part]).astype(bf16)
            ds[all_rows(slot), part] = grad * probs[all_rows(slot), part]
        part = dot(ds[all_rows(slot), :], q_hat[...])
        if slot == levels:
            own[KEY] = part
        else:
            give(slot, KEY, part)

    per_head = tokens // chunk
    for index, part in enumerate(parts):
        h = index // per_head
        rows_here = slice(part.start - h * tokens, part.stop - h * tokens)
        columns = slice(h * head, (h + 1) * head)
        grad_t = dot(k_hat_t[...], ds[:, part]) * (scale_row[:, part] * score_scale)
        dq_ref[rows_here, columns] = jnp.transpose(grad_t.astype(bf16))
        out_ref[rows_here, columns] = jnp.transpose(attended[index])
    relay(KEY)

    for kind, target in ((VALUE, dv_ref), (KEY, dk_ref)):
        for piece, span in enumerate(spans):
            for level in (GROUP, FAR):
                wait_part(level, kind, piece)
            total_part = own[kind][span]
            for level, mine in (
                (NEAR, in_ring < RING - 1), (TWO, in_ring < RING - 2), (GROUP, has_next(GROUP)),
                (PAIR, core == 0), (FAR, has_next(FAR)),
            ):
                total_part = total_part + chosen(mine, level, kind, span)
            target[span, :] = total_part.astype(bf16)
    pair_sent = jnp.logical_or(core == 0, relays_pair)
    for kind, piece in pieces:
        for level in range(levels):
            sent = {GROUP: has_next(GROUP), FAR: has_next(FAR), PAIR: pair_sent}.get(level, True)
            if level == TWO:
                sent = in_ring < RING - 1 if kind == KEY else False
            back = True if level in (NEAR, TWO, PAIR) else has_prev(level)
            for condition, copy in (
                (sent, forward_copy(level, kind, piece, kv)), (back, back_copy(level, kind, piece))
            ):
                if condition is True:
                    copy.wait_send()
                elif condition is not False:
                    pl.when(condition)(copy.wait_send)
        pl.when(in_ring == RING - 2 if kind == KEY else in_ring >= 0)(
            via_copy(kind, piece, kv).wait_send
        )
        pl.when(in_ring == 1 if kind == KEY else in_ring >= 0)(last_copy(kind, piece).wait_send)


def deliver(*refs):
    count = (len(refs) - 2) // 3
    sources, targets, held = refs[:count], refs[count : 2 * count], refs[2 * count : 3 * count]
    load_sem, store_sem = refs[3 * count :]
    loads = [pltpu.make_async_copy(sources[i], held[i], load_sem.at[i]) for i in range(count)]
    stores = [pltpu.make_async_copy(held[i], targets[i], store_sem.at[i]) for i in range(count)]
    for load in loads:
        load.start()
    for load, store in zip(loads, stores):
        load.wait()
        store.start()
    for store in stores:
        store.wait()


def local(rows, cols, queries, key_rows, value_rows, out_grad, link_mask):
    tokens, head = key_rows.shape
    heads = queries.shape[1] // head
    levels = link_mask.shape[1]
    width = heads * tokens
    sources = levels + 1
    dma = pltpu.SemaphoreType.DMA
    vmem = pl.BlockSpec(memory_space=pltpu.VMEM)
    hbm = pl.BlockSpec(memory_space=pl.ANY)
    results = pl.pallas_call(
        functools.partial(kernel, rows, cols, levels, min(256, tokens)),
        out_shape=(
            jax.ShapeDtypeStruct(queries.shape, bf16),
            jax.ShapeDtypeStruct(queries.shape, bf16),
            jax.ShapeDtypeStruct(key_rows.shape, bf16),
            jax.ShapeDtypeStruct(value_rows.shape, bf16),
        ),
        in_specs=[hbm, hbm, hbm, hbm, pl.BlockSpec(memory_space=pltpu.SMEM)],
        out_specs=(vmem, vmem, vmem, vmem),
        scratch_shapes=[
            pltpu.VMEM(queries.shape, bf16),
            pltpu.VMEM(queries.shape, bf16),
            pltpu.VMEM((2, tokens, head), bf16),
            pltpu.VMEM((levels, 2, tokens, head), bf16),
            pltpu.VMEM((2, tokens, head), bf16),
            pltpu.VMEM((levels, 2, tokens, head), bf16),
            pltpu.VMEM((levels, 2, tokens, head), bf16),
            pltpu.VMEM((2, tokens, head), f32),
            pltpu.VMEM((tokens, 2 * head), bf16),
            pltpu.VMEM((2 * head, width), bf16),
            pltpu.VMEM((width, head), bf16),
            pltpu.VMEM((width, head), bf16),
            pltpu.VMEM((2 * head, width), bf16),
            pltpu.VMEM((head, sources * tokens), bf16),
            pltpu.VMEM((head, sources * tokens), bf16),
            pltpu.VMEM((sources * tokens, width), f32),
            pltpu.VMEM((sources * tokens, width), bf16),
            pltpu.VMEM((sources * tokens, width), bf16),
            pltpu.VMEM((sources, 8, width), f32),
            dma((4,)),
            dma((levels, 2, HALVES)),
            dma((levels, 2, HALVES)),
            dma((2, HALVES)),
            dma((2, HALVES)),
            dma((2, HALVES)),
            dma((levels, 2, HALVES)),
            dma((levels, 2, HALVES)),
        ],
        compiler_params=pltpu.CompilerParams(
            collective_id=0, has_side_effects=True, vmem_limit_bytes=60 * 2**20
        ),
    )(queries, key_rows, value_rows, out_grad, link_mask)
    return pl.pallas_call(
        deliver,
        out_shape=tuple(jax.ShapeDtypeStruct(each.shape, each.dtype) for each in results),
        in_specs=[hbm] * len(results),
        out_specs=(hbm,) * len(results),
        scratch_shapes=[pltpu.VMEM(each.shape, each.dtype) for each in results]
        + [dma((len(results),))] * 2,
        compiler_params=pltpu.CompilerParams(vmem_limit_bytes=60 * 2**20),
    )(*results)


def solution(mesh):
    spec = P(("row", "col"), None)
    return jax.shard_map(
        functools.partial(local, mesh.shape["row"], mesh.shape["col"]),
        mesh=mesh,
        in_specs=(spec,) * 5,
        out_specs=(spec,) * 4,
        check_vma=False,
    )
```

```python
import functools
import math

import jax
import jax.numpy as jnp
from jax import lax
from jax.experimental import pallas as pl
from jax.experimental.pallas import tpu as pltpu
from jax.sharding import PartitionSpec as P

scale_eps = 1e-06
MESH = pl.DeviceIdType.MESH
bf16 = jnp.bfloat16
f32 = jnp.float32
RING = 4
NEAR, TWO, GROUP, PAIR, FAR = range(5)
KEY, VALUE = 0, 1
PIECES = 2


def quantize(values):
    largest = jnp.max(jnp.abs(values), axis=1, keepdims=True)
    scales = (largest + scale_eps).astype(bf16).astype(f32)
    codes = jnp.clip(jnp.floor(values * (127.0 / scales) + 0.5), -127.0, 127.0)
    return codes, scales


def dot(left, right):
    return jnp.dot(left, right, preferred_element_type=f32)


def kernel(
    rows, cols, levels, chunk,
    q_hbm, k_hbm, v_hbm, g_hbm, link_ref,
    out_hbm, dq_hbm, dk_hbm, dv_hbm,
    out_ref, dq_ref, dk_ref, dv_ref,
    q_ref, g_ref, kv, kv_in, via, part_out, part_in, held,
    keys, q_codes_t, q_hat, g_rows, g_aug_t, k_hat_t, values_t, scores, probs, ds, tops,
    load_sem, store_sem, send_fwd, recv_fwd, send_via, recv_via, send_hop, send_bwd, recv_bwd,
):
    tokens, head = k_hbm.shape
    heads = q_hbm.shape[1] // head
    width = heads * tokens
    blocks = rows * cols
    block_id = lax.axis_index("row") * cols + lax.axis_index("col")
    score_scale = 1.0 / math.sqrt(head)
    in_ring = lax.rem(block_id, RING)
    ring_start = block_id - in_ring
    core = lax.rem(block_id // 8, 2)
    distances = [2**level for level in range(levels)]

    def place(block):
        return (block // cols, lax.rem(block, cols))

    def ring(steps):
        return ring_start + lax.rem(in_ring + steps, RING)

    partner = block_id + 8 - 16 * core
    ahead = [ring(1), ring(2), block_id + 4, partner, block_id + 16]
    behind = [ring(3), ring(2), block_id - 4, partner, block_id - 16]

    loads = []
    for index, (source, target) in enumerate(
        ((k_hbm, kv.at[KEY]), (v_hbm, kv.at[VALUE]), (q_hbm, q_ref), (g_hbm, g_ref))
    ):
        copy = pltpu.make_async_copy(source, target, load_sem.at[index])
        copy.start()
        loads.append(copy)

    stores = [
        pltpu.make_async_copy(source, target, store_sem.at[index])
        for index, (source, target) in enumerate(
            ((out_ref, out_hbm), (dq_ref, dq_hbm), (dv_ref, dv_hbm), (dk_ref, dk_hbm))
        )
    ]

    def has_next(level):
        return block_id + distances[level] < blocks

    def has_prev(level):
        return block_id >= distances[level]

    barrier = pltpu.get_barrier_semaphore()

    def greet(block):
        pl.semaphore_signal(barrier, inc=1, device_id=place(block), device_id_type=MESH)

    for level in (FAR, GROUP):
        pl.when(has_next(level))(functools.partial(greet, ahead[level]))
        pl.when(has_prev(level))(functools.partial(greet, behind[level]))
    for other in (ring(1), ring(2), ring(3), partner):
        greet(other)

    for level in range(GROUP, levels):
        @pl.when(jnp.logical_not(has_prev(level)))
        def _():
            kv_in[level] = jnp.zeros(kv_in.shape[1:], bf16)

    for level in (GROUP, FAR):
        @pl.when(jnp.logical_not(has_next(level)))
        def _():
            part_in[level] = jnp.zeros(part_in.shape[1:], bf16)

    met = sum(has(level).astype(jnp.int32) for level in (GROUP, FAR) for has in (has_next, has_prev))
    for copy in loads[:2]:
        copy.wait()
    pl.semaphore_wait(barrier, 4 + met)

    half = tokens // PIECES
    pieces = [(kind, piece) for kind in (KEY, VALUE) for piece in range(PIECES)]

    def forward_copy(level, kind, piece, source):
        span = pl.ds(piece * half, half)
        return pltpu.make_async_remote_copy(
            src_ref=source.at[kind, span],
            dst_ref=kv_in.at[level, kind, span],
            send_sem=send_fwd.at[level, kind, piece],
            recv_sem=recv_fwd.at[level, kind, piece],
            device_id=place(ahead[level]),
            device_id_type=MESH,
        )

    def hop_copy(kind, piece, source, steps, sent):
        span = pl.ds(piece * half, half)
        return pltpu.make_async_remote_copy(
            src_ref=source.at[span],
            dst_ref=kv_in.at[TWO, kind, span],
            send_sem=sent,
            recv_sem=recv_fwd.at[TWO, kind, piece],
            device_id=place(ring(steps)),
            device_id_type=MESH,
        )

    def near_copy(piece):
        return hop_copy(KEY, piece, kv_in.at[NEAR, KEY], 1, send_fwd.at[TWO, KEY, piece])

    def last_copy(kind, piece):
        return hop_copy(kind, piece, via.at[kind], RING - 1, send_hop.at[kind, piece])

    def via_copy(kind, piece, source):
        span = pl.ds(piece * half, half)
        return pltpu.make_async_remote_copy(
            src_ref=source.at[kind, span],
            dst_ref=via.at[kind, span],
            send_sem=send_via.at[kind, piece],
            recv_sem=recv_via.at[kind, piece],
            device_id=place(ring(RING - 1)),
            device_id_type=MESH,
        )

    def pass_near(condition, piece):
        @pl.when(condition)
        def _():
            wait_rows(NEAR, KEY, piece)

        @pl.when(jnp.logical_and(condition, in_ring < RING - 1))
        def _():
            near_copy(piece).start()

    def pass_via(kind, piece):
        @pl.when(in_ring == 1 if kind == KEY else in_ring >= 0)
        def _():
            via_copy(kind, piece, kv).wait_recv()
            last_copy(kind, piece).start()

    def send_rows(condition, level, kind, piece, source):
        @pl.when(condition)
        def _():
            forward_copy(level, kind, piece, source).start()

    def wait_rows(level, kind, piece):
        if level < GROUP:
            forward_copy(level, kind, piece, kv).wait_recv()
        else:
            @pl.when(has_prev(level))
            def _():
                forward_copy(level, kind, piece, kv).wait_recv()

    relays_pair = jnp.logical_and(core == 1, has_prev(FAR))
    for kind, piece in pieces:
        send_rows(has_next(GROUP), GROUP, kind, piece, kv)
        send_rows(has_next(FAR), FAR, kind, piece, kv)
        if kind == VALUE:
            pl.when(in_ring < RING - 2)(via_copy(kind, piece, kv).start)
        send_rows(in_ring < RING - 1, NEAR, kind, piece, kv)
        send_rows(core == 0, PAIR, kind, piece, kv)

    def pass_far(kind, piece):
        wait_rows(FAR, kind, piece)
        send_rows(relays_pair, PAIR, kind, piece, kv_in.at[FAR])

    def pass_group(kind, piece):
        wait_rows(GROUP, kind, piece)
        send_rows(in_ring >= RING - 1, NEAR, kind, piece, kv_in.at[GROUP])
        late = in_ring == RING - 2 if kind == KEY else in_ring >= RING - 2
        pl.when(late)(via_copy(kind, piece, kv_in.at[GROUP]).start)

    for copy in loads[2:]:
        copy.wait()
    row_factors = []
    for h in range(heads):
        span = pl.ds(h * tokens, tokens)
        codes, scales = quantize(q_ref[:, h * head : (h + 1) * head].astype(f32))
        q_hat[span, :] = (codes * (scales / 127.0)).astype(bf16)
        codes_t = jnp.transpose(codes.astype(bf16))
        q_codes_t[:head, span] = codes_t
        q_codes_t[head:, span] = codes_t
        factor = scales * (1.0 / (127.0 * 127.0 * math.sqrt(head))) * (1.0 / math.log(2.0))
        row_factors.append(jnp.transpose(jnp.broadcast_to(factor, (tokens, head)))[:1, :])
        g_head = g_ref[:, h * head : (h + 1) * head]
        g_aug_t[:head, span] = jnp.transpose(g_head)
    row_factor = jnp.concatenate(row_factors, axis=1)
    g_aug_t[head:, :] = jnp.zeros((head, width), bf16)

    def rows_of(slot):
        return kv if slot == levels else kv_in.at[slot]

    def fold(values, reduce):
        return reduce(values.reshape(-1, 8, values.shape[1]), axis=0)

    def all_rows(slot):
        return slice(slot * tokens, (slot + 1) * tokens)

    parts = [slice(start, start + chunk) for start in range(0, width, chunk)]

    def score(slot):
        codes, scales = quantize(rows_of(slot)[KEY].astype(f32))
        span = slice(slot * tokens, (slot + 1) * tokens)
        k_hat_t[:, span] = jnp.transpose((codes * (scales / 127.0)).astype(bf16))
        scaled = codes * scales
        high = scaled.astype(bf16)
        keys[:, :head] = high
        keys[:, head:] = (scaled - high.astype(f32)).astype(bf16)
        for part in parts:
            raw = dot(keys[...], q_codes_t[:, part])
            if slot == levels:
                key_at = lax.broadcasted_iota(jnp.int32, raw.shape, 0)
                query_at = lax.broadcasted_iota(jnp.int32, raw.shape, 1) + part.start % tokens
                raw = jnp.where(key_at <= query_at, raw, -jnp.inf)
            scores[span, part] = raw
            tops[slot, :, part] = fold(raw, jnp.max)

    score(levels)
    early = jnp.logical_or(in_ring == 1, in_ring == 2)
    for piece in range(PIECES):
        pass_near(early, piece)
    for piece in range(PIECES):
        pass_group(KEY, piece)
        pass_far(KEY, piece)
    score(GROUP)
    for piece in range(PIECES):
        pass_near(jnp.logical_not(early), piece)
        pass_via(KEY, piece)
    for piece in range(PIECES // 2):
        pass_group(VALUE, piece)
        pass_far(VALUE, piece)
    score(FAR)
    for piece in range(PIECES // 2, PIECES):
        pass_group(VALUE, piece)
        pass_far(VALUE, piece)
    score(NEAR)
    for piece in range(PIECES // 2):
        pass_via(VALUE, piece)
    for piece in range(PIECES):
        wait_rows(PAIR, KEY, piece)
    score(PAIR)
    for piece in range(PIECES // 2, PIECES):
        pass_via(VALUE, piece)
    for piece in range(PIECES):
        wait_rows(TWO, KEY, piece)
    score(TWO)
    order = (PAIR, TWO, NEAR, FAR, GROUP, levels)

    allowed = [
        jnp.logical_and(has_prev(level), link_ref[0, level] == 1) for level in range(levels)
    ]
    level_tops = [jnp.max(tops[slot], axis=0, keepdims=True) for slot in range(levels + 1)]
    row_top = level_tops[levels]
    for level in range(levels):
        row_top = jnp.maximum(row_top, jnp.where(allowed[level], level_tops[level], -jnp.inf))
    row_top = row_top * row_factor

    total = jnp.zeros((8, width), f32)
    tile = 128
    for slot in order:
        factor, top = row_factor, row_top
        if slot < levels:
            factor = jnp.where(allowed[slot], factor, 0.0)
            top = jnp.where(allowed[slot], top, 1e30)
        sums = []
        for part in parts:
            acc = jnp.zeros((8, chunk), f32)
            for start in range(slot * tokens, (slot + 1) * tokens, tile):
                span = slice(start, start + tile)
                weights = jnp.exp2(scores[span, part] * factor[:, part] - top[:, part])
                acc = acc + fold(weights, jnp.sum)
                probs[span, part] = weights.astype(bf16)
            sums.append(acc)
        total = total + jnp.concatenate(sums, axis=1)
    scale_row = 1.0 / jnp.sum(total, axis=0, keepdims=True)
    scale_column = jnp.transpose(jnp.broadcast_to(scale_row, (head, width)))
    for h in range(heads):
        span = slice(h * tokens, (h + 1) * tokens)
        g_head = g_ref[:, h * head : (h + 1) * head].astype(f32)
        g_rows[span, :] = (g_head * scale_column[span]).astype(bf16)
    q_hat[...] = (q_hat[...].astype(f32) * (scale_column * score_scale)).astype(bf16)

    def back_copy(level, kind, piece):
        span = pl.ds(piece * half, half)
        return pltpu.make_async_remote_copy(
            src_ref=part_out.at[level, kind, span],
            dst_ref=part_in.at[level, kind, span],
            send_sem=send_bwd.at[level, kind, piece],
            recv_sem=recv_bwd.at[level, kind, piece],
            device_id=place(behind[level]),
            device_id_type=MESH,
        )

    def wait_part(level, kind, piece):
        if level in (GROUP, FAR):
            @pl.when(has_next(level))
            def _():
                back_copy(level, kind, piece).wait_recv()
        else:
            back_copy(level, kind, piece).wait_recv()

    def chosen(condition, level, kind, span=slice(None)):
        return jnp.where(condition, part_in[level, kind, span].astype(f32), 0.0)

    group_sends_now = jnp.logical_and(has_prev(GROUP), in_ring < RING - 2)
    group_relays = jnp.logical_and(has_prev(GROUP), in_ring >= RING - 2)
    spans = [slice(piece * half, (piece + 1) * half) for piece in range(PIECES)]

    def give(level, kind, part):
        if level == GROUP:
            held[kind] = part
        for piece, span in enumerate(spans):
            here = part[span]
            if level == FAR:
                wait_part(PAIR, kind, piece)
                here = here + chosen(core == 1, PAIR, kind, span)
            part_out[level, kind, span] = here.astype(bf16)
            if level in (NEAR, TWO, PAIR):
                back_copy(level, kind, piece).start()
            else:
                @pl.when(has_prev(FAR) if level == FAR else group_sends_now)
                def _():
                    back_copy(level, kind, piece).start()

    def relay(kind):
        for piece, span in enumerate(spans):
            wait_part(TWO, kind, piece)
            wait_part(NEAR, kind, piece)

            @pl.when(group_relays)
            def _():
                part = held[kind, span] + part_in[TWO, kind, span].astype(f32)
                part = part + chosen(in_ring == RING - 1, NEAR, kind, span)
                part_out[GROUP, kind, span] = part.astype(bf16)
                back_copy(GROUP, kind, piece).start()

    own = [None, None]

    for slot in order:
        part = dot(probs[all_rows(slot), :], g_rows[...])
        if slot == levels:
            own[VALUE] = part
        else:
            give(slot, VALUE, part)

    for slot in (PAIR, NEAR, TWO):
        for piece in range(PIECES):
            wait_rows(slot, VALUE, piece)
    for slot in order:
        values_t[:, all_rows(slot)] = jnp.transpose(rows_of(slot)[VALUE])

    attended = []
    for part in parts:
        mixed = dot(values_t[...], probs[:, part])
        attended_t = (mixed * scale_row[:, part]).astype(bf16)
        attended.append(attended_t)
        delta = -jnp.sum(
            g_aug_t[:head, part].astype(f32) * attended_t.astype(f32), axis=0, keepdims=True
        )
        first = delta.astype(bf16).astype(f32)
        second = (delta - first).astype(bf16).astype(f32)
        third = delta - first - second
        row_at = lax.broadcasted_iota(jnp.int32, (16, chunk), 0)
        split = jnp.where(row_at == 0, first, jnp.where(row_at == 1, second, third))
        g_aug_t[head : head + 16, part] = jnp.where(row_at < 3, split, 0.0).astype(bf16)

    ones = jnp.ones((tokens, head), bf16)
    for slot in order:
        if slot == FAR:
            relay(VALUE)
        v_aug = jnp.concatenate([rows_of(slot)[VALUE], ones], axis=1)
        for part in parts:
            grad = dot(v_aug, g_aug_t[:, part]).astype(bf16)
            ds[all_rows(slot), part] = grad * probs[all_rows(slot), part]
        part = dot(ds[all_rows(slot), :], q_hat[...])
        if slot == levels:
            own[KEY] = part
        else:
            give(slot, KEY, part)

    per_head = tokens // chunk
    for index, part in enumerate(parts):
        h = index // per_head
        rows_here = slice(part.start - h * tokens, part.stop - h * tokens)
        columns = slice(h * head, (h + 1) * head)
        grad_t = dot(k_hat_t[...], ds[:, part]) * (scale_row[:, part] * score_scale)
        dq_ref[rows_here, columns] = jnp.transpose(grad_t.astype(bf16))
        out_ref[rows_here, columns] = jnp.transpose(attended[index])
    stores[0].start()
    stores[1].start()
    relay(KEY)

    for kind, target in ((VALUE, dv_ref), (KEY, dk_ref)):
        for piece, span in enumerate(spans):
            for level in (GROUP, FAR):
                wait_part(level, kind, piece)
            total_part = own[kind][span]
            for level, mine in (
                (NEAR, in_ring < RING - 1), (TWO, in_ring < RING - 2), (GROUP, has_next(GROUP)),
                (PAIR, core == 0), (FAR, has_next(FAR)),
            ):
                total_part = total_part + chosen(mine, level, kind, span)
            target[span, :] = total_part.astype(bf16)
        stores[2 if kind == VALUE else 3].start()
    pair_sent = jnp.logical_or(core == 0, relays_pair)
    for kind, piece in pieces:
        for level in range(levels):
            sent = {GROUP: has_next(GROUP), FAR: has_next(FAR), PAIR: pair_sent}.get(level, True)
            if level == TWO:
                sent = in_ring < RING - 1 if kind == KEY else False
            back = True if level in (NEAR, TWO, PAIR) else has_prev(level)
            for condition, copy in (
                (sent, forward_copy(level, kind, piece, kv)), (back, back_copy(level, kind, piece))
            ):
                if condition is True:
                    copy.wait_send()
                elif condition is not False:
                    pl.when(condition)(copy.wait_send)
        pl.when(in_ring == RING - 2 if kind == KEY else in_ring >= 0)(
            via_copy(kind, piece, kv).wait_send
        )
        pl.when(in_ring == 1 if kind == KEY else in_ring >= 0)(last_copy(kind, piece).wait_send)

    for store in stores:
        store.wait()


def deliver(*refs):
    count = (len(refs) - 2) // 3
    sources, targets, held = refs[:count], refs[count : 2 * count], refs[2 * count : 3 * count]
    load_sem, store_sem = refs[3 * count :]
    loads = [pltpu.make_async_copy(sources[i], held[i], load_sem.at[i]) for i in range(count)]
    stores = [pltpu.make_async_copy(held[i], targets[i], store_sem.at[i]) for i in range(count)]
    for load in loads:
        load.start()
    for load, store in zip(loads, stores):
        load.wait()
        store.start()
    for store in stores:
        store.wait()


def local(rows, cols, queries, key_rows, value_rows, out_grad, link_mask):
    tokens, head = key_rows.shape
    heads = queries.shape[1] // head
    levels = link_mask.shape[1]
    width = heads * tokens
    sources = levels + 1
    dma = pltpu.SemaphoreType.DMA
    hbm = pl.BlockSpec(memory_space=pl.ANY)
    results = pl.pallas_call(
        functools.partial(kernel, rows, cols, levels, min(256, tokens)),
        out_shape=(
            jax.ShapeDtypeStruct(queries.shape, bf16),
            jax.ShapeDtypeStruct(queries.shape, bf16),
            jax.ShapeDtypeStruct(key_rows.shape, bf16),
            jax.ShapeDtypeStruct(value_rows.shape, bf16),
        ),
        in_specs=[hbm, hbm, hbm, hbm, pl.BlockSpec(memory_space=pltpu.SMEM)],
        out_specs=(hbm, hbm, hbm, hbm),
        scratch_shapes=[
            pltpu.VMEM(queries.shape, bf16),
            pltpu.VMEM(queries.shape, bf16),
            pltpu.VMEM(key_rows.shape, bf16),
            pltpu.VMEM(value_rows.shape, bf16),
            pltpu.VMEM(queries.shape, bf16),
            pltpu.VMEM(queries.shape, bf16),
            pltpu.VMEM((2, tokens, head), bf16),
            pltpu.VMEM((levels, 2, tokens, head), bf16),
            pltpu.VMEM((2, tokens, head), bf16),
            pltpu.VMEM((levels, 2, tokens, head), bf16),
            pltpu.VMEM((levels, 2, tokens, head), bf16),
            pltpu.VMEM((2, tokens, head), f32),
            pltpu.VMEM((tokens, 2 * head), bf16),
            pltpu.VMEM((2 * head, width), bf16),
            pltpu.VMEM((width, head), bf16),
            pltpu.VMEM((width, head), bf16),
            pltpu.VMEM((2 * head, width), bf16),
            pltpu.VMEM((head, sources * tokens), bf16),
            pltpu.VMEM((head, sources * tokens), bf16),
            pltpu.VMEM((sources * tokens, width), f32),
            pltpu.VMEM((sources * tokens, width), bf16),
            pltpu.VMEM((sources * tokens, width), bf16),
            pltpu.VMEM((sources, 8, width), f32),
            dma((4,)),
            dma((4,)),
            dma((levels, 2, PIECES)),
            dma((levels, 2, PIECES)),
            dma((2, PIECES)),
            dma((2, PIECES)),
            dma((2, PIECES)),
            dma((levels, 2, PIECES)),
            dma((levels, 2, PIECES)),
        ],
        compiler_params=pltpu.CompilerParams(
            collective_id=0, has_side_effects=True, vmem_limit_bytes=60 * 2**20
        ),
    )(queries, key_rows, value_rows, out_grad, link_mask)
    return pl.pallas_call(
        deliver,
        out_shape=tuple(jax.ShapeDtypeStruct(each.shape, each.dtype) for each in results),
        in_specs=[hbm] * len(results),
        out_specs=(hbm,) * len(results),
        scratch_shapes=[pltpu.VMEM(each.shape, each.dtype) for each in results]
        + [dma((len(results),))] * 2,
        compiler_params=pltpu.CompilerParams(vmem_limit_bytes=60 * 2**20),
    )(*results)


def solution(mesh):
    spec = P(("row", "col"), None)
    return jax.shard_map(
        functools.partial(local, mesh.shape["row"], mesh.shape["col"]),
        mesh=mesh,
        in_specs=(spec,) * 5,
        out_specs=(spec,) * 4,
        check_vma=False,
    )
```

```python
import functools
import math

import jax
import jax.numpy as jnp
from jax import lax
from jax.experimental import pallas as pl
from jax.experimental.pallas import tpu as pltpu
from jax.sharding import PartitionSpec as P

scale_eps = 1e-06
MESH = pl.DeviceIdType.MESH
bf16 = jnp.bfloat16
f32 = jnp.float32
RING = 4
NEAR, TWO, GROUP, PAIR, FAR = range(5)
KEY, VALUE = 0, 1
PIECES = 2


def quantize(values):
    largest = jnp.max(jnp.abs(values), axis=1, keepdims=True)
    scales = (largest + scale_eps).astype(bf16).astype(f32)
    codes = jnp.clip(jnp.floor(values * (127.0 / scales) + 0.5), -127.0, 127.0)
    return codes, scales


def dot(left, right):
    return jnp.dot(left, right, preferred_element_type=f32)


def kernel(
    rows, cols, levels, chunk,
    q_hbm, k_hbm, v_hbm, g_hbm, link_ref,
    out_hbm, dq_hbm, dk_hbm, dv_hbm,
    out_ref, dq_ref, dk_ref, dv_ref,
    q_ref, g_ref, kv, kv_in, via, part_out, part_in, held,
    keys, q_codes_t, q_hat, g_rows, g_aug_t, k_hat_t, values_t, scores, probs, ds, tops,
    load_sem, store_sem, send_fwd, recv_fwd, send_via, recv_via, send_hop, send_bwd, recv_bwd,
):
    tokens, head = k_hbm.shape
    heads = q_hbm.shape[1] // head
    width = heads * tokens
    blocks = rows * cols
    block_id = lax.axis_index("row") * cols + lax.axis_index("col")
    score_scale = 1.0 / math.sqrt(head)
    in_ring = lax.rem(block_id, RING)
    ring_start = block_id - in_ring
    core = lax.rem(block_id // 8, 2)
    distances = [2**level for level in range(levels)]

    def place(block):
        return (block // cols, lax.rem(block, cols))

    def ring(steps):
        return ring_start + lax.rem(in_ring + steps, RING)

    partner = block_id + 8 - 16 * core
    ahead = [ring(1), ring(2), block_id + 4, partner, block_id + 16]
    behind = [ring(3), ring(2), block_id - 4, partner, block_id - 16]

    loads = []
    for index, (source, target) in enumerate(
        ((k_hbm, kv.at[KEY]), (v_hbm, kv.at[VALUE]), (q_hbm, q_ref), (g_hbm, g_ref))
    ):
        copy = pltpu.make_async_copy(source, target, load_sem.at[index])
        copy.start()
        loads.append(copy)

    stores = [
        pltpu.make_async_copy(source, target, store_sem.at[index])
        for index, (source, target) in enumerate(
            ((out_ref, out_hbm), (dq_ref, dq_hbm), (dv_ref, dv_hbm), (dk_ref, dk_hbm))
        )
    ]

    def has_next(level):
        return block_id + distances[level] < blocks

    def has_prev(level):
        return block_id >= distances[level]

    barrier = pltpu.get_barrier_semaphore()

    def greet(block):
        pl.semaphore_signal(barrier, inc=1, device_id=place(block), device_id_type=MESH)

    for level in (FAR, GROUP):
        pl.when(has_next(level))(functools.partial(greet, ahead[level]))
        pl.when(has_prev(level))(functools.partial(greet, behind[level]))
    for other in (ring(1), ring(2), ring(3), partner):
        greet(other)

    for level in range(GROUP, levels):
        @pl.when(jnp.logical_not(has_prev(level)))
        def _():
            kv_in[level] = jnp.zeros(kv_in.shape[1:], bf16)

    for level in (GROUP, FAR):
        @pl.when(jnp.logical_not(has_next(level)))
        def _():
            part_in[level] = jnp.zeros(part_in.shape[1:], bf16)

    met = sum(has(level).astype(jnp.int32) for level in (GROUP, FAR) for has in (has_next, has_prev))
    for copy in loads[:2]:
        copy.wait()
    pl.semaphore_wait(barrier, 4 + met)

    half = tokens // PIECES
    pieces = [(kind, piece) for kind in (KEY, VALUE) for piece in range(PIECES)]

    def forward_copy(level, kind, piece, source):
        span = pl.ds(piece * half, half)
        return pltpu.make_async_remote_copy(
            src_ref=source.at[kind, span],
            dst_ref=kv_in.at[level, kind, span],
            send_sem=send_fwd.at[level, kind, piece],
            recv_sem=recv_fwd.at[level, kind, piece],
            device_id=place(ahead[level]),
            device_id_type=MESH,
        )

    def hop_copy(kind, piece, source, steps, sent):
        span = pl.ds(piece * half, half)
        return pltpu.make_async_remote_copy(
            src_ref=source.at[span],
            dst_ref=kv_in.at[TWO, kind, span],
            send_sem=sent,
            recv_sem=recv_fwd.at[TWO, kind, piece],
            device_id=place(ring(steps)),
            device_id_type=MESH,
        )

    def near_copy(piece):
        return hop_copy(KEY, piece, kv_in.at[NEAR, KEY], 1, send_fwd.at[TWO, KEY, piece])

    def last_copy(kind, piece):
        return hop_copy(kind, piece, via.at[kind], RING - 1, send_hop.at[kind, piece])

    def via_copy(kind, piece, source):
        span = pl.ds(piece * half, half)
        return pltpu.make_async_remote_copy(
            src_ref=source.at[kind, span],
            dst_ref=via.at[kind, span],
            send_sem=send_via.at[kind, piece],
            recv_sem=recv_via.at[kind, piece],
            device_id=place(ring(RING - 1)),
            device_id_type=MESH,
        )

    def pass_near(condition, piece):
        @pl.when(condition)
        def _():
            wait_rows(NEAR, KEY, piece)

        @pl.when(jnp.logical_and(condition, in_ring < RING - 1))
        def _():
            near_copy(piece).start()

    def pass_via(kind, piece):
        @pl.when(in_ring == 1 if kind == KEY else in_ring >= 0)
        def _():
            via_copy(kind, piece, kv).wait_recv()
            last_copy(kind, piece).start()

    def send_rows(condition, level, kind, piece, source):
        @pl.when(condition)
        def _():
            forward_copy(level, kind, piece, source).start()

    def wait_rows(level, kind, piece):
        if level < GROUP:
            forward_copy(level, kind, piece, kv).wait_recv()
        else:
            @pl.when(has_prev(level))
            def _():
                forward_copy(level, kind, piece, kv).wait_recv()

    relays_pair = jnp.logical_and(core == 1, has_prev(FAR))
    for kind, piece in pieces:
        send_rows(has_next(GROUP), GROUP, kind, piece, kv)
        send_rows(has_next(FAR), FAR, kind, piece, kv)
        if kind == VALUE:
            pl.when(in_ring < RING - 2)(via_copy(kind, piece, kv).start)
        send_rows(in_ring < RING - 1, NEAR, kind, piece, kv)
        send_rows(core == 0, PAIR, kind, piece, kv)

    def pass_far(kind, piece):
        wait_rows(FAR, kind, piece)
        send_rows(relays_pair, PAIR, kind, piece, kv_in.at[FAR])

    def pass_group(kind, piece):
        wait_rows(GROUP, kind, piece)
        send_rows(in_ring >= RING - 1, NEAR, kind, piece, kv_in.at[GROUP])
        late = in_ring == RING - 2 if kind == KEY else in_ring >= RING - 2
        pl.when(late)(via_copy(kind, piece, kv_in.at[GROUP]).start)

    for copy in loads[2:]:
        copy.wait()
    row_factors = []
    for h in range(heads):
        span = pl.ds(h * tokens, tokens)
        codes, scales = quantize(q_ref[:, h * head : (h + 1) * head].astype(f32))
        q_hat[span, :] = (codes * (scales / 127.0)).astype(bf16)
        codes_t = jnp.transpose(codes.astype(bf16))
        q_codes_t[:head, span] = codes_t
        q_codes_t[head:, span] = codes_t
        factor = scales * (1.0 / (127.0 * 127.0 * math.sqrt(head))) * (1.0 / math.log(2.0))
        row_factors.append(jnp.transpose(jnp.broadcast_to(factor, (tokens, head)))[:1, :])
        g_head = g_ref[:, h * head : (h + 1) * head]
        g_aug_t[:head, span] = jnp.transpose(g_head)
    row_factor = jnp.concatenate(row_factors, axis=1)
    g_aug_t[head:, :] = jnp.zeros((head, width), bf16)

    def rows_of(slot):
        return kv if slot == levels else kv_in.at[slot]

    def fold(values, reduce):
        return reduce(values.reshape(-1, 8, values.shape[1]), axis=0)

    def all_rows(slot):
        return slice(slot * tokens, (slot + 1) * tokens)

    parts = [slice(start, start + chunk) for start in range(0, width, chunk)]

    def score(slot):
        codes, scales = quantize(rows_of(slot)[KEY].astype(f32))
        span = slice(slot * tokens, (slot + 1) * tokens)
        k_hat_t[:, span] = jnp.transpose((codes * (scales / 127.0)).astype(bf16))
        scaled = codes * scales
        high = scaled.astype(bf16)
        keys[:, :head] = high
        keys[:, head:] = (scaled - high.astype(f32)).astype(bf16)
        for part in parts:
            raw = dot(keys[...], q_codes_t[:, part])
            if slot == levels:
                key_at = lax.broadcasted_iota(jnp.int32, raw.shape, 0)
                query_at = lax.broadcasted_iota(jnp.int32, raw.shape, 1) + part.start % tokens
                raw = jnp.where(key_at <= query_at, raw, -jnp.inf)
            scores[span, part] = raw
            tops[slot, :, part] = fold(raw, jnp.max)

    score(levels)
    early = jnp.logical_or(in_ring == 1, in_ring == 2)
    for piece in range(PIECES):
        pass_near(early, piece)
    for piece in range(PIECES):
        pass_group(KEY, piece)
        pass_far(KEY, piece)
    score(GROUP)
    for piece in range(PIECES // 2):
        pass_group(VALUE, piece)
    for piece in range(PIECES):
        pass_near(jnp.logical_not(early), piece)
        pass_via(KEY, piece)
    for piece in range(PIECES // 2):
        pass_far(VALUE, piece)
    score(FAR)
    for piece in range(PIECES // 2, PIECES):
        pass_group(VALUE, piece)
        pass_far(VALUE, piece)
    score(NEAR)
    for piece in range(PIECES // 2):
        pass_via(VALUE, piece)
    for piece in range(PIECES):
        wait_rows(PAIR, KEY, piece)
    score(PAIR)
    for piece in range(PIECES // 2, PIECES):
        pass_via(VALUE, piece)
    for piece in range(PIECES):
        wait_rows(TWO, KEY, piece)
    score(TWO)
    order = (PAIR, TWO, NEAR, FAR, GROUP, levels)

    allowed = [
        jnp.logical_and(has_prev(level), link_ref[0, level] == 1) for level in range(levels)
    ]
    level_tops = [jnp.max(tops[slot], axis=0, keepdims=True) for slot in range(levels + 1)]
    row_top = level_tops[levels]
    for level in range(levels):
        row_top = jnp.maximum(row_top, jnp.where(allowed[level], level_tops[level], -jnp.inf))
    row_top = row_top * row_factor

    total = jnp.zeros((8, width), f32)
    tile = 128
    for slot in order:
        factor, top = row_factor, row_top
        if slot < levels:
            factor = jnp.where(allowed[slot], factor, 0.0)
            top = jnp.where(allowed[slot], top, 1e30)
        sums = []
        for part in parts:
            acc = jnp.zeros((8, chunk), f32)
            for start in range(slot * tokens, (slot + 1) * tokens, tile):
                span = slice(start, start + tile)
                weights = jnp.exp2(scores[span, part] * factor[:, part] - top[:, part])
                acc = acc + fold(weights, jnp.sum)
                probs[span, part] = weights.astype(bf16)
            sums.append(acc)
        total = total + jnp.concatenate(sums, axis=1)
    scale_row = 1.0 / jnp.sum(total, axis=0, keepdims=True)
    scale_column = jnp.transpose(jnp.broadcast_to(scale_row, (head, width)))
    for h in range(heads):
        span = slice(h * tokens, (h + 1) * tokens)
        g_head = g_ref[:, h * head : (h + 1) * head].astype(f32)
        g_rows[span, :] = (g_head * scale_column[span]).astype(bf16)
    q_hat[...] = (q_hat[...].astype(f32) * (scale_column * score_scale)).astype(bf16)

    def back_copy(level, kind, piece):
        span = pl.ds(piece * half, half)
        return pltpu.make_async_remote_copy(
            src_ref=part_out.at[level, kind, span],
            dst_ref=part_in.at[level, kind, span],
            send_sem=send_bwd.at[level, kind, piece],
            recv_sem=recv_bwd.at[level, kind, piece],
            device_id=place(behind[level]),
            device_id_type=MESH,
        )

    def wait_part(level, kind, piece):
        if level in (GROUP, FAR):
            @pl.when(has_next(level))
            def _():
                back_copy(level, kind, piece).wait_recv()
        else:
            back_copy(level, kind, piece).wait_recv()

    def chosen(condition, level, kind, span=slice(None)):
        return jnp.where(condition, part_in[level, kind, span].astype(f32), 0.0)

    group_sends_now = jnp.logical_and(has_prev(GROUP), in_ring < RING - 2)
    group_relays = jnp.logical_and(has_prev(GROUP), in_ring >= RING - 2)
    spans = [slice(piece * half, (piece + 1) * half) for piece in range(PIECES)]

    def give(level, kind, part):
        if level == GROUP:
            held[kind] = part
        for piece, span in enumerate(spans):
            here = part[span]
            if level == FAR:
                wait_part(PAIR, kind, piece)
                here = here + chosen(core == 1, PAIR, kind, span)
            part_out[level, kind, span] = here.astype(bf16)
            if level in (NEAR, TWO, PAIR):
                back_copy(level, kind, piece).start()
            else:
                @pl.when(has_prev(FAR) if level == FAR else group_sends_now)
                def _():
                    back_copy(level, kind, piece).start()

    def relay(kind):
        for piece, span in enumerate(spans):
            wait_part(TWO, kind, piece)
            wait_part(NEAR, kind, piece)

            @pl.when(group_relays)
            def _():
                part = held[kind, span] + part_in[TWO, kind, span].astype(f32)
                part = part + chosen(in_ring == RING - 1, NEAR, kind, span)
                part_out[GROUP, kind, span] = part.astype(bf16)
                back_copy(GROUP, kind, piece).start()

    own = [None, None]

    for slot in order:
        part = dot(probs[all_rows(slot), :], g_rows[...])
        if slot == levels:
            own[VALUE] = part
        else:
            give(slot, VALUE, part)

    for slot in (PAIR, NEAR, TWO):
        for piece in range(PIECES):
            wait_rows(slot, VALUE, piece)
    for slot in order:
        values_t[:, all_rows(slot)] = jnp.transpose(rows_of(slot)[VALUE])

    attended = []
    for part in parts:
        mixed = dot(values_t[...], probs[:, part])
        attended_t = (mixed * scale_row[:, part]).astype(bf16)
        attended.append(attended_t)
        delta = -jnp.sum(
            g_aug_t[:head, part].astype(f32) * attended_t.astype(f32), axis=0, keepdims=True
        )
        first = delta.astype(bf16).astype(f32)
        second = (delta - first).astype(bf16).astype(f32)
        third = delta - first - second
        row_at = lax.broadcasted_iota(jnp.int32, (16, chunk), 0)
        split = jnp.where(row_at == 0, first, jnp.where(row_at == 1, second, third))
        g_aug_t[head : head + 16, part] = jnp.where(row_at < 3, split, 0.0).astype(bf16)

    ones = jnp.ones((tokens, head), bf16)
    for slot in order:
        if slot == FAR:
            relay(VALUE)
        v_aug = jnp.concatenate([rows_of(slot)[VALUE], ones], axis=1)
        for part in parts:
            grad = dot(v_aug, g_aug_t[:, part]).astype(bf16)
            ds[all_rows(slot), part] = grad * probs[all_rows(slot), part]
        part = dot(ds[all_rows(slot), :], q_hat[...])
        if slot == levels:
            own[KEY] = part
        else:
            give(slot, KEY, part)

    per_head = tokens // chunk
    for index, part in enumerate(parts):
        h = index // per_head
        rows_here = slice(part.start - h * tokens, part.stop - h * tokens)
        columns = slice(h * head, (h + 1) * head)
        grad_t = dot(k_hat_t[...], ds[:, part]) * (scale_row[:, part] * score_scale)
        dq_ref[rows_here, columns] = jnp.transpose(grad_t.astype(bf16))
        out_ref[rows_here, columns] = jnp.transpose(attended[index])
    stores[0].start()
    stores[1].start()
    relay(KEY)

    for kind, target in ((VALUE, dv_ref), (KEY, dk_ref)):
        for piece, span in enumerate(spans):
            for level in (GROUP, FAR):
                wait_part(level, kind, piece)
            total_part = own[kind][span]
            for level, mine in (
                (NEAR, in_ring < RING - 1), (TWO, in_ring < RING - 2), (GROUP, has_next(GROUP)),
                (PAIR, core == 0), (FAR, has_next(FAR)),
            ):
                total_part = total_part + chosen(mine, level, kind, span)
            target[span, :] = total_part.astype(bf16)
        stores[2 if kind == VALUE else 3].start()
    pair_sent = jnp.logical_or(core == 0, relays_pair)
    for kind, piece in pieces:
        for level in range(levels):
            sent = {GROUP: has_next(GROUP), FAR: has_next(FAR), PAIR: pair_sent}.get(level, True)
            if level == TWO:
                sent = in_ring < RING - 1 if kind == KEY else False
            back = True if level in (NEAR, TWO, PAIR) else has_prev(level)
            for condition, copy in (
                (sent, forward_copy(level, kind, piece, kv)), (back, back_copy(level, kind, piece))
            ):
                if condition is True:
                    copy.wait_send()
                elif condition is not False:
                    pl.when(condition)(copy.wait_send)
        pl.when(in_ring == RING - 2 if kind == KEY else in_ring >= 0)(
            via_copy(kind, piece, kv).wait_send
        )
        pl.when(in_ring == 1 if kind == KEY else in_ring >= 0)(last_copy(kind, piece).wait_send)

    for store in stores:
        store.wait()


def deliver(*refs):
    count = (len(refs) - 2) // 3
    sources, targets, held = refs[:count], refs[count : 2 * count], refs[2 * count : 3 * count]
    load_sem, store_sem = refs[3 * count :]
    loads = [pltpu.make_async_copy(sources[i], held[i], load_sem.at[i]) for i in range(count)]
    stores = [pltpu.make_async_copy(held[i], targets[i], store_sem.at[i]) for i in range(count)]
    for load in loads:
        load.start()
    for load, store in zip(loads, stores):
        load.wait()
        store.start()
    for store in stores:
        store.wait()


def local(rows, cols, queries, key_rows, value_rows, out_grad, link_mask):
    tokens, head = key_rows.shape
    heads = queries.shape[1] // head
    levels = link_mask.shape[1]
    width = heads * tokens
    sources = levels + 1
    dma = pltpu.SemaphoreType.DMA
    hbm = pl.BlockSpec(memory_space=pl.ANY)
    results = pl.pallas_call(
        functools.partial(kernel, rows, cols, levels, min(256, tokens)),
        out_shape=(
            jax.ShapeDtypeStruct(queries.shape, bf16),
            jax.ShapeDtypeStruct(queries.shape, bf16),
            jax.ShapeDtypeStruct(key_rows.shape, bf16),
            jax.ShapeDtypeStruct(value_rows.shape, bf16),
        ),
        in_specs=[hbm, hbm, hbm, hbm, pl.BlockSpec(memory_space=pltpu.SMEM)],
        out_specs=(hbm, hbm, hbm, hbm),
        scratch_shapes=[
            pltpu.VMEM(queries.shape, bf16),
            pltpu.VMEM(queries.shape, bf16),
            pltpu.VMEM(key_rows.shape, bf16),
            pltpu.VMEM(value_rows.shape, bf16),
            pltpu.VMEM(queries.shape, bf16),
            pltpu.VMEM(queries.shape, bf16),
            pltpu.VMEM((2, tokens, head), bf16),
            pltpu.VMEM((levels, 2, tokens, head), bf16),
            pltpu.VMEM((2, tokens, head), bf16),
            pltpu.VMEM((levels, 2, tokens, head), bf16),
            pltpu.VMEM((levels, 2, tokens, head), bf16),
            pltpu.VMEM((2, tokens, head), f32),
            pltpu.VMEM((tokens, 2 * head), bf16),
            pltpu.VMEM((2 * head, width), bf16),
            pltpu.VMEM((width, head), bf16),
            pltpu.VMEM((width, head), bf16),
            pltpu.VMEM((2 * head, width), bf16),
            pltpu.VMEM((head, sources * tokens), bf16),
            pltpu.VMEM((head, sources * tokens), bf16),
            pltpu.VMEM((sources * tokens, width), f32),
            pltpu.VMEM((sources * tokens, width), bf16),
            pltpu.VMEM((sources * tokens, width), bf16),
            pltpu.VMEM((sources, 8, width), f32),
            dma((4,)),
            dma((4,)),
            dma((levels, 2, PIECES)),
            dma((levels, 2, PIECES)),
            dma((2, PIECES)),
            dma((2, PIECES)),
            dma((2, PIECES)),
            dma((levels, 2, PIECES)),
            dma((levels, 2, PIECES)),
        ],
        compiler_params=pltpu.CompilerParams(
            collective_id=0, has_side_effects=True, vmem_limit_bytes=60 * 2**20
        ),
    )(queries, key_rows, value_rows, out_grad, link_mask)
    return pl.pallas_call(
        deliver,
        out_shape=tuple(jax.ShapeDtypeStruct(each.shape, each.dtype) for each in results),
        in_specs=[hbm] * len(results),
        out_specs=(hbm,) * len(results),
        scratch_shapes=[pltpu.VMEM(each.shape, each.dtype) for each in results]
        + [dma((len(results),))] * 2,
        compiler_params=pltpu.CompilerParams(vmem_limit_bytes=60 * 2**20),
    )(*results)


def solution(mesh):
    spec = P(("row", "col"), None)
    return jax.shard_map(
        functools.partial(local, mesh.shape["row"], mesh.shape["col"]),
        mesh=mesh,
        in_specs=(spec,) * 5,
        out_specs=(spec,) * 4,
        check_vma=False,
    )
```
